128 devices in a mesh: samp: 16 (over y, x), par: 8 (over z, core).
Axes of the slice: x: 4, y: 4, z: 4, core: 2. Of those that a mesh axis runs over, the one named last changes fastest.
Arguments:
- log_derivs: bfloat16 [1024, 524288], P('samp', 'par')
- energies: float32 [1024, 8], P('samp'), may hold values from -6 to 6
- nys_rows: int32 [16, 8], P('samp'), may hold values from 0 to 63, as said below
Outputs:
- update: float32 [524288, 8], P('par')
- solution: float32 [1024, 8], P('samp')
The draws below stay inside these ranges and needn't reach their ends.
Inputs may be any that keep to these rules, and one draw needn't show every extreme that they name: `nys_rows`: each row holds 8 different local sample numbers of that group.
All inputs are finite; a program needn't handle non-finite values.
Results may differ from the reference program's by a relative error of at most 0.014.
Values may be sent and summed in bfloat16 or wider, within the bound.
No kernel may reach another device: no remote copies, remote signals or barrier semaphores. Data moves between devices by JAX's collectives and lax.ppermute only.
A program may use at most 128 MiB of HBM per device.

```python
import math
import jax
import jax.numpy as jnp
from jax import lax

SAMP_DEV = 64
PAR_DEV = 65536
NV = 8
RANK_DEV = 8
ITERS = 2
GROUPS = 16
NS = 1024
NP = 524288
RANK = 128
N_PAR = 8


def draw_log_derivs(key, part):
    subkeys = jax.random.split(jax.random.fold_in(key, 11), 6)
    row_scale = jnp.exp(jax.random.uniform(subkeys[0], (NS, 1), jnp.float32, 0.0, math.log(10.0)))
    col_scale = jnp.exp(jax.random.uniform(subkeys[1], (1, NP), jnp.float32, math.log(0.5), math.log(2.0)))
    offset = 2.0 * jax.random.normal(subkeys[2], (1, NP), jnp.float32)
    latent_count = max(NS // 8, 8)
    latent = jax.random.normal(subkeys[4], (NS, latent_count), jnp.float32)
    loading = jax.random.normal(subkeys[5], (latent_count, NP), jnp.float32) * (0.5 / math.sqrt(latent_count))
    shared = jnp.dot(latent, loading)
    fluctuation = jax.random.normal(subkeys[3], (NS, NP), jnp.float32)
    return (offset + row_scale * (col_scale * fluctuation + shared)).astype(jnp.bfloat16)


def draw_nys_rows(key, part):
    subkeys = jax.random.split(jax.random.fold_in(key, 7), GROUPS)

    def pick_rows(subkey):
        return jax.random.permutation(subkey, SAMP_DEV)[:RANK_DEV]
    return jax.vmap(pick_rows)(subkeys).astype(jnp.int32)


def block_levels(own_key, extent, cuts, low, top_value):
    factor_of, own = 1.0, jax.random.fold_in(own_key, 6)
    for position, shards_of in cuts:
        heights = jnp.exp(jax.random.uniform(jax.random.fold_in(own, position), (shards_of,), jnp.float32, low / len(cuts), top_value / len(cuts)))
        factor_of = factor_of * jnp.repeat(heights, extent[position] // shards_of).reshape([-1 if axis == position else 1 for axis in range(len(extent))])
    return factor_of


def scatter_about(stream_key, extent, spread, bound, cuts=(), kind=jnp.bfloat16):
    gain = block_levels(stream_key, extent, cuts, -0.22, 0.18) if cuts else 1.0
    drawn = jax.random.normal(stream_key, extent, jnp.float32) * spread * gain
    return jnp.minimum(jnp.maximum(drawn, -bound), bound).astype(kind)


def setup_inputs(seed: int = 0) -> dict:
    splits = jax.random.split(jax.random.key(seed), 4)
    log_derivs = draw_log_derivs(jax.random.fold_in(splits[3], 71), 0)
    energies = scatter_about(splits[1], (NS, NV), 1.0, 6.0, ((0, 16),), jnp.float32)
    nys_rows = draw_nys_rows(jax.random.fold_in(splits[3], 71), 0)
    return {"log_derivs": log_derivs, "energies": energies, "nys_rows": nys_rows}


damping = 0.5

def centered_block(log_derivs, index):
    block = lax.dynamic_slice_in_dim(log_derivs, (index * PAR_DEV).astype(jnp.int32), PAR_DEV, 1).astype(jnp.float32)
    column_mean = lax.optimization_barrier(jnp.sum(block, axis=0)) / NS
    return ((block - column_mean) * (1.0 / math.sqrt(NP))).astype(jnp.bfloat16)

def factor_solve(factor, right):
    middle = lax.linalg.triangular_solve(factor, right, left_side=True, lower=True)
    return lax.linalg.triangular_solve(factor, middle, left_side=True, lower=True, transpose_a=True)

def small_solve(matrix, right):
    return factor_solve(jnp.linalg.cholesky(matrix), right)

def hdot(left, right):
    return jnp.dot(left, right, precision=lax.Precision.HIGHEST)

def reference(log_derivs, energies, nys_rows):
    selected = (jnp.arange(GROUPS, dtype=jnp.int32)[:, None] * SAMP_DEV + nys_rows).reshape(-1).astype(jnp.int32)
    indices = jnp.arange(N_PAR, dtype=jnp.int32)

    def add_sketch(total, index):
        block = centered_block(log_derivs, index)
        chosen = jnp.take(block, selected, axis=0)
        return (total + jnp.dot(block.astype(jnp.float32), chosen.T.astype(jnp.float32), preferred_element_type=jnp.float32), None)
    sketch, unused = lax.scan(add_sketch, jnp.zeros((NS, RANK), jnp.float32), indices)
    core_block = jnp.take(sketch, selected, axis=0)
    inner_matrix = damping * core_block + hdot(sketch.T, sketch)
    factor = jnp.linalg.cholesky(inner_matrix)

    def precondition(residual):
        coeffs = factor_solve(factor, hdot(sketch.T, residual))
        result = (residual - hdot(sketch, coeffs)) / damping
        return (result, hdot(result.T, residual))

    def apply_kernel(direction):
        rounded = direction.astype(jnp.bfloat16)

        def add_image(total, index):
            block = centered_block(log_derivs, index)
            projected = jnp.dot(block.T.astype(jnp.float32), rounded.astype(jnp.float32), preferred_element_type=jnp.float32)
            return (total + hdot(block.astype(jnp.float32), projected), None)
        images, unused_two = lax.scan(add_image, jnp.zeros((NS, NV), jnp.float32), indices)
        return images + damping * direction
    solution = jnp.zeros((NS, NV), jnp.float32)
    residual = energies
    precond_res, inner_prev = precondition(residual)
    direction = precond_res
    for iteration in range(ITERS):
        image_k = apply_kernel(direction)
        curvature = hdot(direction.T, image_k)
        alpha_k = small_solve(curvature, inner_prev)
        solution = solution + hdot(direction, alpha_k)
        if iteration + 1 < ITERS:
            residual = residual - hdot(image_k, alpha_k)
            precond_res, inner_next = precondition(residual)
            beta_k = small_solve(inner_prev, inner_next)
            direction = precond_res + hdot(direction, beta_k)
            inner_prev = inner_next
    rounded_sol = solution.astype(jnp.bfloat16)

    def update_block(index):
        block = centered_block(log_derivs, index)
        return jnp.dot(block.T.astype(jnp.float32), rounded_sol.astype(jnp.float32), preferred_element_type=jnp.float32)
    update = lax.map(update_block, indices).reshape(NP, NV)
    return (update, solution)
```

```python
import functools
import math

import jax
import jax.numpy as jnp
from jax import lax
from jax.experimental import pallas as pl
from jax.experimental.pallas import tpu as pltpu
from jax.sharding import Mesh
from jax.sharding import PartitionSpec as P

DAMPING = 0.5
SAMP = ("y", "x")
PAR = ("z", "c")
EVERY = ("y", "x", "z", "c")
F32 = jnp.float32
BF16 = jnp.bfloat16
HIGH = lax.Precision.HIGHEST


def mul_nn(a, b, precision=None):
    return lax.dot_general(a, b, (((1,), (0,)), ((), ())), precision=precision, preferred_element_type=F32)


def mul_nt(a, b, precision=None):
    return lax.dot_general(a, b, (((1,), (1,)), ((), ())), precision=precision, preferred_element_type=F32)


def mul_tn(a, b, precision=None):
    return lax.dot_general(a, b, (((0,), (0,)), ((), ())), precision=precision, preferred_element_type=F32)


def shift(value, axis, by):
    n = lax.axis_size(axis)
    return lax.ppermute(value, axis, [(i, (i + by) % n) for i in range(n)])


def sum_axis(value, axis):
    n = lax.axis_size(axis)
    if n == 2:
        return value + shift(value, axis, 1)
    one, two, three = shift(value, axis, 1), shift(value, axis, 2), shift(value, axis, 3)
    return (value + two) + (one + three)


def sum_everywhere(value):
    for axis in ("c", "x", "y", "z"):
        value = sum_axis(value, axis)
    return value


def gather_ring(value, axis):
    n = lax.axis_size(axis)
    parts = jnp.stack([value] + [shift(value, axis, -by) for by in range(1, n)])
    start = lax.rem(n - lax.axis_index(axis), n)
    return lax.dynamic_slice_in_dim(jnp.concatenate([parts, parts]), start, n, 0)


def eliminate(cols, right, rows):
    b = len(cols)
    cols = list(cols)
    for j in range(b):
        col = cols[j]
        inv = 1.0 / col[j : j + 1, :]
        line = right[j : j + 1, :] * inv
        right = jnp.where(rows == j, line, right - col * line)
        for m in range(j + 1, b):
            line = cols[m][j : j + 1, :] * inv
            cols[m] = jnp.where(rows == j, line, cols[m] - col * line)
    return right


def solve_small(matrix, right):
    b = matrix.shape[0]
    rows = lax.broadcasted_iota(jnp.int32, right.shape, 0)
    cols = [jnp.broadcast_to(matrix[:, m : m + 1], right.shape) for m in range(b)]
    return eliminate(cols, right, rows)


def negative_inverse(a, b=16):
    n = a.shape[0]
    rows = lax.broadcasted_iota(jnp.int32, (b, n), 0)
    lanes = lax.broadcasted_iota(jnp.int32, (b, n), 1)
    all_rows = lax.broadcasted_iota(jnp.int32, (n, n), 0)
    all_lanes = lax.broadcasted_iota(jnp.int32, (n, n), 1)
    for k in range(0, n, b):
        panel = a[k : k + b, :]
        inside = (lanes >= k) & (lanes < k + b)
        left = jnp.where(inside, jnp.where(lanes == rows + k, 1.0, 0.0), panel)
        cols = [jnp.broadcast_to(panel[:, k + m : k + m + 1], (b, n)) for m in range(b)]
        right = eliminate(cols, left, rows)
        touched = ((all_rows >= k) & (all_rows < k + b)) | ((all_lanes >= k) & (all_lanes < k + b))
        a = jnp.where(touched, 0.0, a) - mul_tn(left, right, HIGH)
    return a


def gram_kernel(scale, sel_ref, x_ref, c_ref, hi_ref, lo_ref, sketch_ref, acc_ref):
    step = pl.program_id(0)
    rows = x_ref.shape[0]
    x = x_ref[...].astype(F32)
    mean = jnp.sum(x, axis=0, keepdims=True) / rows
    centered = ((x - mean) * scale).astype(BF16)
    c_ref[...] = centered
    product = mul_nt(centered, centered)

    @pl.when(step == 0)
    def _():
        acc_ref[...] = product

    @pl.when(step > 0)
    def _():
        acc_ref[...] += product

    @pl.when(step == pl.num_programs(0) - 1)
    def _():
        high = acc_ref[...].astype(BF16)
        hi_ref[...] = high
        lo_ref[...] = (acc_ref[...] - high.astype(F32)).astype(BF16)
        for j in range(sketch_ref.shape[0]):
            sketch_ref[pl.ds(j, 1), :] = acc_ref[pl.ds(sel_ref[j], 1), :]


def gram_call(selected, slab, scale):
    rows, cols = slab.shape
    rank = selected.shape[0]
    width = min(512, cols)
    whole = lambda i, s: (0, 0)
    return pl.pallas_call(
        functools.partial(gram_kernel, scale),
        grid_spec=pltpu.PrefetchScalarGridSpec(
            num_scalar_prefetch=1,
            grid=(cols // width,),
            in_specs=[pl.BlockSpec((rows, width), lambda i, s: (0, i))],
            out_specs=[
                pl.BlockSpec((rows, width), lambda i, s: (0, i)),
                pl.BlockSpec((rows, rows), whole),
                pl.BlockSpec((rows, rows), whole),
                pl.BlockSpec((rank, rows), whole),
            ],
            scratch_shapes=[pltpu.VMEM((rows, rows), F32)],
        ),
        out_shape=[
            jax.ShapeDtypeStruct((rows, cols), BF16),
            jax.ShapeDtypeStruct((rows, rows), BF16),
            jax.ShapeDtypeStruct((rows, rows), BF16),
            jax.ShapeDtypeStruct((rank, rows), F32),
        ],
        compiler_params=pltpu.CompilerParams(vmem_limit_bytes=48 * 1024 * 1024),
        name="gram",
    )(selected, slab)


def precondition(residual, sketch, neg_inv):
    coeffs = mul_nn(mul_nt(residual, sketch, HIGH), neg_inv, HIGH)
    result = (residual + mul_nn(coeffs, sketch, HIGH)) / DAMPING
    return result, mul_nt(result, residual, HIGH)


def local_image(direction, hi_ref, lo_ref):
    rounded = direction.astype(BF16)
    return mul_nn(rounded, hi_ref[...]) + mul_nn(rounded, lo_ref[...])


def first_kernel(sel_ref, sketch_ref, e_ref, hi_ref, lo_ref, inv_ref, d_ref, gamma_ref, image_ref):
    sketch = sketch_ref[...]
    lanes = lax.broadcasted_iota(jnp.int32, sketch.shape, 1)
    picked = jnp.where(lanes == sel_ref[...], DAMPING, 0.0)
    neg_inv = negative_inverse(mul_nt(sketch, sketch + picked, HIGH))
    inv_ref[...] = neg_inv
    direction, gamma = precondition(e_ref[...], sketch, neg_inv)
    d_ref[...] = direction
    gamma_ref[...] = gamma
    image_ref[...] = local_image(direction, hi_ref, lo_ref)


def second_kernel(
    sum_ref, d_ref, e_ref, inv_ref, sketch_ref, gamma_ref, hi_ref, lo_ref, d1_ref, alpha_ref, gamma1_ref, curv_ref
):
    direction, gamma = d_ref[...], gamma_ref[...]
    image = sum_ref[...] + DAMPING * direction
    alpha = solve_small(mul_nt(direction, image, HIGH), gamma)
    alpha_ref[...] = alpha
    residual = e_ref[...] - mul_tn(alpha, image, HIGH)
    result, gamma1 = precondition(residual, sketch_ref[...], inv_ref[...])
    gamma1_ref[...] = gamma1
    direction1 = result + mul_tn(solve_small(gamma, gamma1), direction, HIGH)
    d1_ref[...] = direction1
    curv_ref[...] = mul_nt(direction1, local_image(direction1, hi_ref, lo_ref), HIGH)


def last_kernel(curv_ref, d_ref, d1_ref, alpha_ref, gamma1_ref, p0_ref, p1_ref, solution_ref, update_ref):
    d1, alpha = d1_ref[...], alpha_ref[...]
    curvature = curv_ref[...] + DAMPING * mul_nt(d1, d1, HIGH)
    alpha1 = solve_small(curvature, gamma1_ref[...])
    solution_ref[...] = mul_tn(alpha, d_ref[...], HIGH) + mul_tn(alpha1, d1, HIGH)
    update_ref[...] = (mul_tn(alpha, p0_ref[...], HIGH) + mul_tn(alpha1, p1_ref[...], HIGH)).astype(update_ref.dtype)


def call(kernel, name, outs, *args):
    return pl.pallas_call(
        kernel,
        out_shape=[jax.ShapeDtypeStruct(shape, dtype) for shape, dtype in outs],
        compiler_params=pltpu.CompilerParams(vmem_limit_bytes=40 * 1024 * 1024),
        name=name,
    )(*args)


def body(log_derivs, energies, nys_rows):
    samp_rows, nv = energies.shape
    per_group = nys_rows.shape[1]
    groups = lax.axis_size(SAMP)
    n = samp_rows * groups
    rank = per_group * groups
    total_cols = log_derivs.shape[1] * lax.axis_size(PAR)

    small = jnp.concatenate(
        [
            energies.T,
            nys_rows.astype(F32).T,
            jnp.zeros((nv, 128 - samp_rows - 1), F32),
        ],
        axis=1,
    )
    small = gather_ring(gather_ring(small, "x"), "y").reshape(groups, nv, 128)
    e = jnp.moveaxis(small[:, :, :samp_rows], 0, 1).reshape(nv, n)
    picks = small[:, :, samp_rows].astype(jnp.int32)
    selected = (jnp.arange(groups, dtype=jnp.int32)[:, None] * samp_rows + picks).reshape(-1)

    slab = lax.all_to_all(log_derivs, SAMP, split_axis=1, concat_axis=0, tiled=True)
    centered, high, low, sketch = gram_call(selected, slab, 1.0 / math.sqrt(total_cols))

    pieces = sketch.reshape(rank // 8, 8, n // 128, 128).swapaxes(1, 2).reshape(-1, 8, 128)
    own = jnp.sum(lax.all_to_all(pieces, EVERY, 0, 0, tiled=True), axis=0)
    pieces = lax.all_to_all(jnp.broadcast_to(own[None], pieces.shape), EVERY, 0, 0, tiled=True)
    sketch = pieces.reshape(rank // 8, n // 128, 8, 128).swapaxes(1, 2).reshape(rank, n)

    vec, mat = ((nv, n), F32), ((nv, nv), F32)
    neg_inv, d0, gamma0, image = call(
        first_kernel, "first", [((rank, rank), F32), vec, mat, vec], selected[:, None], sketch, e, high, low
    )
    p0 = mul_nn(d0.astype(BF16), centered)
    image = sum_everywhere(image)
    d1, alpha0, gamma1, curvature = call(
        second_kernel, "second", [vec, mat, mat, mat], image, d0, e, neg_inv, sketch, gamma0, high, low
    )
    p1 = mul_nn(d1.astype(BF16), centered)
    curvature = sum_everywhere(curvature)
    solution, update = call(
        last_kernel, "last", [vec, (p0.shape, BF16)], curvature, d0, d1, alpha0, gamma1, p0, p1
    )
    blocks = lax.all_to_all(jnp.broadcast_to(update[None], (groups, *update.shape)), SAMP, 0, 0, tiled=True)
    update = jnp.moveaxis(blocks.astype(F32), 0, 1).reshape(nv, -1).T
    start = lax.axis_index(SAMP) * samp_rows
    return update, lax.dynamic_slice_in_dim(solution, start, samp_rows, 1).T


def solution(mesh):
    finer = Mesh(mesh.devices.reshape(4, 4, 4, 2), EVERY)
    in_specs = (P(SAMP, PAR), P(SAMP, None), P(SAMP, None))
    out_specs = (P(PAR, None), P(SAMP, None))
    return jax.shard_map(body, mesh=finer, in_specs=in_specs, out_specs=out_specs, check_vma=False)
```

```python
import functools
import math

import jax
import jax.numpy as jnp
from jax import lax
from jax.experimental import pallas as pl
from jax.experimental.pallas import tpu as pltpu
from jax.sharding import Mesh
from jax.sharding import PartitionSpec as P

DAMPING = 0.5
SAMP = ("y", "x")
PAR = ("z", "c")
EVERY = ("y", "x", "z", "c")
F32 = jnp.float32
BF16 = jnp.bfloat16
HIGH = lax.Precision.HIGHEST


def mul_nn(a, b, precision=None):
    return lax.dot_general(a, b, (((1,), (0,)), ((), ())), precision=precision, preferred_element_type=F32)


def mul_nt(a, b, precision=None):
    return lax.dot_general(a, b, (((1,), (1,)), ((), ())), precision=precision, preferred_element_type=F32)


def mul_tn(a, b, precision=None):
    return lax.dot_general(a, b, (((0,), (0,)), ((), ())), precision=precision, preferred_element_type=F32)


def shift(value, axis, by):
    n = lax.axis_size(axis)
    return lax.ppermute(value, axis, [(i, (i + by) % n) for i in range(n)])


def sum_axis(value, axis):
    n = lax.axis_size(axis)
    if n == 2:
        return value + shift(value, axis, 1)
    one, two, three = shift(value, axis, 1), shift(value, axis, 2), shift(value, axis, 3)
    return (value + two) + (one + three)


def sum_everywhere(value):
    for axis in ("c", "x", "y", "z"):
        value = sum_axis(value, axis)
    return value


def eliminate(cols, right, rows):
    b = len(cols)
    cols = list(cols)
    for j in range(b):
        col = cols[j]
        inv = 1.0 / col[j : j + 1, :]
        line = right[j : j + 1, :] * inv
        right = jnp.where(rows == j, line, right - col * line)
        for m in range(j + 1, b):
            line = cols[m][j : j + 1, :] * inv
            cols[m] = jnp.where(rows == j, line, cols[m] - col * line)
    return right


def solve_small(matrix, right):
    b = matrix.shape[0]
    rows = lax.broadcasted_iota(jnp.int32, right.shape, 0)
    cols = [jnp.broadcast_to(matrix[:, m : m + 1], right.shape) for m in range(b)]
    return eliminate(cols, right, rows)


def negative_inverse(a, b=16):
    n = a.shape[0]
    rows = lax.broadcasted_iota(jnp.int32, (b, n), 0)
    lanes = lax.broadcasted_iota(jnp.int32, (b, n), 1)
    all_rows = lax.broadcasted_iota(jnp.int32, (n, n), 0)
    all_lanes = lax.broadcasted_iota(jnp.int32, (n, n), 1)
    for k in range(0, n, b):
        panel = a[k : k + b, :]
        inside = (lanes >= k) & (lanes < k + b)
        left = jnp.where(inside, jnp.where(lanes == rows + k, 1.0, 0.0), panel)
        cols = [jnp.broadcast_to(panel[:, k + m : k + m + 1], (b, n)) for m in range(b)]
        right = eliminate(cols, left, rows)
        touched = ((all_rows >= k) & (all_rows < k + b)) | ((all_lanes >= k) & (all_lanes < k + b))
        a = jnp.where(touched, 0.0, a) - mul_tn(left, right, HIGH)
    return a


def pack_kernel(l_ref, extra_ref, out_ref, buffer, sems):
    parts = buffer.shape[0]
    width = l_ref.shape[1] // parts
    loads = [
        pltpu.make_async_copy(
            l_ref.at[:, pl.ds(i * width, width)], buffer.at[i, :, pl.ds(0, width)], sems.at[0, i]
        )
        for i in range(parts)
    ]
    stores = [pltpu.make_async_copy(buffer.at[i], out_ref.at[i], sems.at[1, i]) for i in range(parts)]
    for load in loads:
        load.start()
    for i in range(parts):
        buffer[i, :, width:] = extra_ref[...]
    for load, store in zip(loads, stores):
        load.wait()
        store.start()
    for store in stores:
        store.wait()


def pack(local, parts, extra):
    rows, cols = local.shape[0], local.shape[1] // parts
    shape = (parts, rows, cols + extra.shape[1])
    return pl.pallas_call(
        pack_kernel,
        in_specs=[pl.BlockSpec(memory_space=pl.ANY), pl.BlockSpec(memory_space=pltpu.VMEM)],
        out_specs=pl.BlockSpec(memory_space=pl.ANY),
        out_shape=jax.ShapeDtypeStruct(shape, BF16),
        scratch_shapes=[pltpu.VMEM(shape, BF16), pltpu.SemaphoreType.DMA((2, parts))],
        compiler_params=pltpu.CompilerParams(vmem_limit_bytes=60 * 1024 * 1024),
        name="pack",
    )(local, extra)


def selection(sel_ref, groups, n):
    rank = sel_ref.shape[0]
    ranks = lax.broadcasted_iota(jnp.int32, (rank, n), 0)
    lanes = lax.broadcasted_iota(jnp.int32, (rank, n), 1)
    return lanes == (ranks // (rank // groups)) * (n // groups) + sel_ref[...]


def sketch_kernel(scale, sel_ref, slab_ref, c_ref, sketch_ref, pick_ref, acc_ref):
    step = pl.program_id(0)
    groups, rows, _ = slab_ref.shape
    n = groups * rows

    @pl.when(step == 0)
    def _():
        pick_ref[...] = jnp.where(selection(sel_ref, groups, n), 1.0, 0.0).astype(BF16)
        acc_ref[...] = jnp.zeros_like(acc_ref)

    total = 0.0
    for i in range(groups):
        total = total + jnp.sum(slab_ref[i].astype(F32), axis=0, keepdims=True)
    mean = total / n
    for i in range(groups):
        c_ref[i * rows : (i + 1) * rows, :] = ((slab_ref[i].astype(F32) - mean) * scale).astype(BF16)
    chosen = mul_nn(pick_ref[...], c_ref[...]).astype(BF16)
    acc_ref[...] += mul_nt(chosen, c_ref[...])

    @pl.when(step == pl.num_programs(0) - 1)
    def _():
        for i in range(0, acc_ref.shape[0], 8):
            for j in range(0, n, 128):
                sketch_ref[i * n // 1024 + j // 128] = acc_ref[i : i + 8, j : j + 128]


def sketch_call(selected, slab, cols, scale):
    groups, rows, _ = slab.shape
    rank, n = selected.shape[0], groups * rows
    width = min(512, cols)
    return pl.pallas_call(
        functools.partial(sketch_kernel, scale),
        grid=(cols // width,),
        in_specs=[
            pl.BlockSpec((rank, 1), lambda i: (0, 0)),
            pl.BlockSpec((groups, rows, width), lambda i: (0, 0, i)),
        ],
        out_specs=[
            pl.BlockSpec((n, width), lambda i: (0, i)),
            pl.BlockSpec((rank * n // 1024, 8, 128), lambda i: (0, 0, 0)),
        ],
        out_shape=[
            jax.ShapeDtypeStruct((n, cols), BF16),
            jax.ShapeDtypeStruct((rank * n // 1024, 8, 128), F32),
        ],
        scratch_shapes=[pltpu.VMEM((rank, n), BF16), pltpu.VMEM((rank, n), F32)],
        compiler_params=pltpu.CompilerParams(vmem_limit_bytes=58 * 1024 * 1024),
        name="sketch",
    )(selected, slab)


def gram_kernel(c_ref, hi_ref, lo_ref, acc_ref):
    step = pl.program_id(0)
    n = c_ref.shape[0]
    block = n // 4
    for i in range(0, n, block):
        product = mul_nt(c_ref[i : i + block, :], c_ref[...])

        @pl.when(step == 0)
        def _():
            acc_ref[i : i + block, :] = product

        @pl.when(step > 0)
        def _():
            acc_ref[i : i + block, :] += product

    @pl.when(step == pl.num_programs(0) - 1)
    def _():
        high = acc_ref[...].astype(BF16)
        hi_ref[...] = high
        lo_ref[...] = (acc_ref[...] - high.astype(F32)).astype(BF16)


def gram(centered):
    n, cols = centered.shape
    width = min(1024, cols)
    whole = lambda i: (0, 0)
    return pl.pallas_call(
        gram_kernel,
        grid=(cols // width,),
        in_specs=[pl.BlockSpec((n, width), lambda i: (0, i))],
        out_specs=[pl.BlockSpec((n, n), whole)] * 2,
        out_shape=[jax.ShapeDtypeStruct((n, n), BF16)] * 2,
        scratch_shapes=[pltpu.VMEM((n, n), F32)],
        compiler_params=pltpu.CompilerParams(vmem_limit_bytes=58 * 1024 * 1024),
        cost_estimate=pl.CostEstimate(flops=2 * n * n * cols, bytes_accessed=2 * n * cols, transcendentals=0),
        name="gram",
    )(centered)


def project_kernel(d0_ref, d1_ref, slab_ref, out_ref):
    rounded = jnp.concatenate([d0_ref[...], d1_ref[...]]).astype(BF16)
    out_ref[...] = mul_nn(rounded, slab_ref[...])


def project(d0, d1, centered):
    n, cols = centered.shape
    width = min(1024, cols)
    whole = pl.BlockSpec(d0.shape, lambda i: (0, 0))
    return pl.pallas_call(
        project_kernel,
        grid=(cols // width,),
        in_specs=[whole, whole, pl.BlockSpec((n, width), lambda i: (0, i))],
        out_specs=pl.BlockSpec((2 * d0.shape[0], width), lambda i: (0, i)),
        out_shape=jax.ShapeDtypeStruct((2 * d0.shape[0], cols), F32),
        cost_estimate=pl.CostEstimate(flops=32 * n * cols, bytes_accessed=2 * n * cols, transcendentals=0),
        compiler_params=pltpu.CompilerParams(vmem_limit_bytes=58 * 1024 * 1024),
        name="project",
    )(d0, d1, centered)


def precondition(residual, sketch, neg_inv):
    coeffs = mul_nn(mul_nt(residual, sketch, HIGH), neg_inv, HIGH)
    result = (residual + mul_nn(coeffs, sketch, HIGH)) / DAMPING
    return result, mul_nt(result, residual, HIGH)


def local_image(direction, hi_ref, lo_ref):
    rounded = direction.astype(BF16)
    return mul_nn(rounded, hi_ref[...]) + mul_nn(rounded, lo_ref[...])


def first_kernel(groups, sel_ref, sketch_ref, e_ref, hi_ref, lo_ref, inv_ref, d_ref, gamma_ref, image_ref):
    sketch = sketch_ref[...]
    picked = jnp.where(selection(sel_ref, groups, sketch.shape[1]), DAMPING, 0.0)
    neg_inv = negative_inverse(mul_nt(sketch, sketch + picked, HIGH))
    inv_ref[...] = neg_inv
    direction, gamma = precondition(e_ref[...], sketch, neg_inv)
    d_ref[...] = direction
    gamma_ref[...] = gamma
    image_ref[...] = local_image(direction, hi_ref, lo_ref)


def second_kernel(
    sum_ref, d_ref, e_ref, inv_ref, sketch_ref, gamma_ref, hi_ref, lo_ref, d1_ref, alpha_ref, gamma1_ref, curv_ref
):
    direction, gamma = d_ref[...], gamma_ref[...]
    image = sum_ref[...] + DAMPING * direction
    alpha = solve_small(mul_nt(direction, image, HIGH), gamma)
    alpha_ref[...] = alpha
    residual = e_ref[...] - mul_tn(alpha, image, HIGH)
    result, gamma1 = precondition(residual, sketch_ref[...], inv_ref[...])
    gamma1_ref[...] = gamma1
    direction1 = result + mul_tn(solve_small(gamma, gamma1), direction, HIGH)
    d1_ref[...] = direction1
    curvature = mul_nt(direction1, local_image(direction1, hi_ref, lo_ref), HIGH)
    nv = curvature.shape[0]
    flat = jnp.concatenate([curvature[i : i + 1, :] for i in range(nv)] + [jnp.zeros((1, 128 - nv * nv), F32)], axis=1)
    curv_ref[...] = jnp.broadcast_to(flat[None], curv_ref.shape)


def last_kernel(curv_ref, d_ref, d1_ref, alpha_ref, gamma1_ref, projected_ref, solution_ref, update_ref):
    d1, alpha = d1_ref[...], alpha_ref[...]
    nv = alpha.shape[0]
    flat = jnp.sum(curv_ref[...], axis=0)
    curvature = jnp.concatenate([flat[:, nv * i : nv * i + nv] for i in range(nv)])
    curvature = curvature + DAMPING * mul_nt(d1, d1, HIGH)
    alpha1 = solve_small(curvature, gamma1_ref[...])
    solution_ref[...] = mul_tn(alpha, d_ref[...], HIGH) + mul_tn(alpha1, d1, HIGH)
    update = mul_tn(jnp.concatenate([alpha, alpha1]), projected_ref[...], HIGH).astype(update_ref.dtype)
    for i in range(update_ref.shape[0]):
        update_ref[i] = update


def call(kernel, name, outs, *args):
    return pl.pallas_call(
        kernel,
        out_shape=[jax.ShapeDtypeStruct(shape, dtype) for shape, dtype in outs],
        compiler_params=pltpu.CompilerParams(vmem_limit_bytes=24 * 1024 * 1024),
        name=name,
    )(*args)


def body(log_derivs, energies, nys_rows):
    samp_rows, nv = energies.shape
    per_group = nys_rows.shape[1]
    groups = lax.axis_size(SAMP)
    n = samp_rows * groups
    rank = per_group * groups
    devices = lax.axis_size(EVERY)
    total_cols = log_derivs.shape[1] * lax.axis_size(PAR)

    upper = energies.astype(BF16)
    left = energies - upper.astype(F32)
    middle = left.astype(BF16)
    lower = (left - middle.astype(F32)).astype(BF16)
    numbers = jnp.pad(nys_rows.astype(BF16).T, ((0, samp_rows - per_group), (0, 127 - 3 * nv)))
    extra = jnp.concatenate([upper, middle, lower, numbers], axis=1)

    cols = log_derivs.shape[1] // groups
    slab = lax.all_to_all(pack(log_derivs, groups, extra), SAMP, 0, 0, tiled=True)
    extras = slab[:, :, cols:].astype(F32)
    e = extras[:, :, :nv] + (extras[:, :, nv : 2 * nv] + extras[:, :, 2 * nv : 3 * nv])
    e = jnp.moveaxis(e, 2, 0).reshape(nv, n)
    picks = extras[:, :per_group, 3 * nv].astype(jnp.int32).reshape(rank, 1)
    centered, pieces = sketch_call(picks, slab, cols, 1.0 / math.sqrt(total_cols))
    high, low = gram(centered)

    got = lax.all_to_all(pieces, EVERY, 0, 0, tiled=True)
    got, high, low, e = lax.optimization_barrier((got, high, low, e))
    own = jnp.sum(got, axis=0)
    pieces = lax.all_to_all(jnp.broadcast_to(own[None], pieces.shape), EVERY, 0, 0, tiled=True)
    sketch = pieces.reshape(rank // 8, n // 128, 8, 128).swapaxes(1, 2).reshape(rank, n)

    vec, mat = ((nv, n), F32), ((nv, nv), F32)
    neg_inv, d0, gamma0, image = call(
        functools.partial(first_kernel, groups), "first", [((rank, rank), F32), vec, mat, vec], picks, sketch, e, high, low
    )
    image = sum_everywhere(image)
    d1, alpha0, gamma1, curvature = call(
        second_kernel, "second", [vec, mat, mat, ((devices, 1, 128), F32)], image, d0, e, neg_inv, sketch, gamma0, high, low
    )
    curvature = lax.all_to_all(curvature, EVERY, 0, 0, tiled=True)
    projected = project(d0, d1, centered)
    solution, update = call(
        last_kernel, "last", [vec, ((groups, nv, cols), BF16)], curvature, d0, d1, alpha0, gamma1, projected
    )
    blocks = lax.all_to_all(update, SAMP, 0, 0, tiled=True)
    update = jnp.moveaxis(blocks.astype(F32), 0, 1).reshape(nv, -1).T
    start = lax.axis_index(SAMP) * samp_rows
    return update, lax.dynamic_slice_in_dim(solution, start, samp_rows, 1).T


def solution(mesh):
    finer = Mesh(mesh.devices.reshape(4, 4, 4, 2), EVERY)
    in_specs = (P(SAMP, PAR), P(SAMP, None), P(SAMP, None))
    out_specs = (P(PAR, None), P(SAMP, None))
    return jax.shard_map(body, mesh=finer, in_specs=in_specs, out_specs=out_specs, check_vma=False)
```

```python
import functools
import math

import jax
import jax.numpy as jnp
from jax import lax
from jax.experimental import pallas as pl
from jax.experimental.pallas import tpu as pltpu
from jax.sharding import Mesh
from jax.sharding import PartitionSpec as P

DAMPING = 0.5
SAMP = ("y", "x")
PAR = ("z", "c")
EVERY = ("y", "x", "z", "c")
F32 = jnp.float32
BF16 = jnp.bfloat16
HIGH = lax.Precision.HIGHEST


def mul_nn(a, b, precision=None):
    return lax.dot_general(a, b, (((1,), (0,)), ((), ())), precision=precision, preferred_element_type=F32)


def mul_nt(a, b, precision=None):
    return lax.dot_general(a, b, (((1,), (1,)), ((), ())), precision=precision, preferred_element_type=F32)


def mul_tn(a, b, precision=None):
    return lax.dot_general(a, b, (((0,), (0,)), ((), ())), precision=precision, preferred_element_type=F32)


def shift(value, axis, by):
    n = lax.axis_size(axis)
    return lax.ppermute(value, axis, [(i, (i + by) % n) for i in range(n)])


def sum_axis(value, axis):
    n = lax.axis_size(axis)
    if n == 2:
        return value + shift(value, axis, 1)
    one, two, three = shift(value, axis, 1), shift(value, axis, 2), shift(value, axis, 3)
    return (value + two) + (one + three)


def sum_everywhere(value):
    for axis in ("c", "x", "y", "z"):
        value = sum_axis(value, axis)
    return value


def eliminate(cols, right, rows):
    b = len(cols)
    cols = list(cols)
    for j in range(b):
        col = cols[j]
        inv = 1.0 / col[j : j + 1, :]
        line = right[j : j + 1, :] * inv
        right = jnp.where(rows == j, line, right - col * line)
        for m in range(j + 1, b):
            line = cols[m][j : j + 1, :] * inv
            cols[m] = jnp.where(rows == j, line, cols[m] - col * line)
    return right


def solve_small(matrix, right):
    b = matrix.shape[0]
    rows = lax.broadcasted_iota(jnp.int32, right.shape, 0)
    cols = [jnp.broadcast_to(matrix[:, m : m + 1], right.shape) for m in range(b)]
    return eliminate(cols, right, rows)


def negative_inverse(a, b=16):
    n = a.shape[0]
    rows = lax.broadcasted_iota(jnp.int32, (b, n), 0)
    lanes = lax.broadcasted_iota(jnp.int32, (b, n), 1)
    all_rows = lax.broadcasted_iota(jnp.int32, (n, n), 0)
    all_lanes = lax.broadcasted_iota(jnp.int32, (n, n), 1)
    for k in range(0, n, b):
        panel = a[k : k + b, :]
        inside = (lanes >= k) & (lanes < k + b)
        left = jnp.where(inside, jnp.where(lanes == rows + k, 1.0, 0.0), panel)
        cols = [jnp.broadcast_to(panel[:, k + m : k + m + 1], (b, n)) for m in range(b)]
        right = eliminate(cols, left, rows)
        touched = ((all_rows >= k) & (all_rows < k + b)) | ((all_lanes >= k) & (all_lanes < k + b))
        a = jnp.where(touched, 0.0, a) - mul_tn(left, right, HIGH)
    return a


def pack_kernel(l_ref, e_ref, picks_ref, out_ref, sems):
    parts, rows, width = out_ref.shape
    width -= 128
    loads = [
        pltpu.make_async_copy(
            l_ref.at[:, pl.ds(i * width, width)], out_ref.at[i, :, pl.ds(0, width)], sems.at[i]
        )
        for i in range(parts)
    ]
    for load in loads:
        load.start()
    e = e_ref[...]
    nv, group_rows = e.shape
    upper = e.astype(BF16).astype(F32)
    middle = (e - upper).astype(BF16).astype(F32)
    lower = e - upper - middle
    square = (picks_ref.shape[1],) * 2
    diagonal = lax.broadcasted_iota(jnp.int32, square, 0) == lax.broadcasted_iota(jnp.int32, square, 1)
    picks = jnp.broadcast_to(picks_ref[...].astype(F32), square)
    picks = jnp.sum(jnp.where(diagonal, picks, 0.0), axis=1, keepdims=True)
    side = (nv, 128 - group_rows)
    picks = jnp.where(lax.broadcasted_iota(jnp.int32, side, 1) == 0, picks, 0.0)
    none = jnp.zeros(side, F32)
    tile = jnp.concatenate(
        [
            jnp.concatenate([upper, picks], axis=1),
            jnp.concatenate([middle, none], axis=1),
            jnp.concatenate([lower, none], axis=1),
            jnp.zeros((rows - 3 * nv, 128), F32),
        ]
    ).astype(BF16)
    for i in range(parts):
        out_ref[i, :, width:] = tile
    for load in loads:
        load.wait()


def pack(local, parts, energies, picks):
    rows, cols = local.shape[0], local.shape[1] // parts
    vmem = pl.BlockSpec(memory_space=pltpu.VMEM)
    return pl.pallas_call(
        pack_kernel,
        in_specs=[pl.BlockSpec(memory_space=pl.ANY), vmem, vmem],
        out_specs=vmem,
        out_shape=jax.ShapeDtypeStruct((parts, rows, cols + 128), BF16),
        scratch_shapes=[pltpu.SemaphoreType.DMA((parts,))],
        compiler_params=pltpu.CompilerParams(vmem_limit_bytes=48 * 1024 * 1024),
        name="pack",
    )(local, energies, picks)


def selection(sel_ref, n):
    return lax.broadcasted_iota(jnp.int32, (sel_ref.shape[0], n), 1) == sel_ref[...]


def sketch_kernel(scale, slab_ref, c_ref, sketch_ref, e_ref, sel_ref, pick_ref, acc_ref):
    groups, rows, _ = slab_ref.shape
    n, cols = c_ref.shape
    nv = e_ref.shape[0]
    for i in range(groups):
        tile = slab_ref[i, 0:32, cols:].astype(F32)
        upper, middle, lower = tile[0:nv], tile[nv : 2 * nv], tile[2 * nv : 3 * nv]
        e_ref[:, i * rows : (i + 1) * rows] = (upper + (middle + lower))[:, :rows]
        sel_ref[i * nv : (i + 1) * nv, :] = upper[:, rows : rows + 1].astype(jnp.int32) + i * rows
    pick_ref[...] = jnp.where(selection(sel_ref, n), 1.0, 0.0).astype(BF16)
    width = min(512, cols)
    for start in range(0, cols, width):
        place = slice(start, start + width)
        total = 0.0
        for i in range(groups):
            total = total + jnp.sum(slab_ref[i, :, place].astype(F32), axis=0, keepdims=True)
        mean = total / n
        for i in range(groups):
            c_ref[i * rows : (i + 1) * rows, place] = ((slab_ref[i, :, place].astype(F32) - mean) * scale).astype(BF16)
        chosen = mul_nn(pick_ref[...], c_ref[:, place]).astype(BF16)
        product = mul_nt(chosen, c_ref[:, place])
        acc_ref[...] = product if start == 0 else acc_ref[...] + product
    for i in range(0, acc_ref.shape[0], 8):
        for j in range(0, n, 128):
            sketch_ref[i * n // 1024 + j // 128] = acc_ref[i : i + 8, j : j + 128]


def sketch_call(slab, cols, nv, per_group, scale):
    groups, rows, _ = slab.shape
    rank, n = per_group * groups, groups * rows
    return pl.pallas_call(
        functools.partial(sketch_kernel, scale),
        in_specs=[pl.BlockSpec(memory_space=pltpu.VMEM)],
        out_specs=[pl.BlockSpec(memory_space=pltpu.VMEM)] * 4,
        out_shape=[
            jax.ShapeDtypeStruct((n, cols), BF16),
            jax.ShapeDtypeStruct((rank * n // 1024, 8, 128), F32),
            jax.ShapeDtypeStruct((nv, n), F32),
            jax.ShapeDtypeStruct((rank, 1), jnp.int32),
        ],
        scratch_shapes=[pltpu.VMEM((rank, n), BF16), pltpu.VMEM((rank, n), F32)],
        compiler_params=pltpu.CompilerParams(vmem_limit_bytes=24 * 1024 * 1024),
        name="sketch",
    )(slab)


def gram_kernel(c_ref, hi_ref, lo_ref):
    n = c_ref.shape[0]
    block = n // 4
    for i in range(0, n, block):
        product = mul_nt(c_ref[i : i + block, :], c_ref[...])
        high = product.astype(BF16)
        hi_ref[i : i + block, :] = high
        lo_ref[i : i + block, :] = (product - high.astype(F32)).astype(BF16)


def gram(centered):
    n, cols = centered.shape
    return pl.pallas_call(
        gram_kernel,
        in_specs=[pl.BlockSpec(memory_space=pltpu.VMEM)],
        out_specs=[pl.BlockSpec(memory_space=pltpu.VMEM)] * 2,
        out_shape=[jax.ShapeDtypeStruct((n, n), BF16)] * 2,
        compiler_params=pltpu.CompilerParams(vmem_limit_bytes=24 * 1024 * 1024),
        cost_estimate=pl.CostEstimate(flops=2 * n * n * cols, bytes_accessed=2 * n * cols, transcendentals=0),
        name="gram",
    )(centered)


def project_kernel(d0_ref, d1_ref, slab_ref, out_ref):
    rounded = jnp.concatenate([d0_ref[...], d1_ref[...]]).astype(BF16)
    out_ref[...] = mul_nn(rounded, slab_ref[...])


def precondition(residual, sketch, neg_inv):
    coeffs = mul_nn(mul_nt(residual, sketch, HIGH), neg_inv, HIGH)
    result = (residual + mul_nn(coeffs, sketch, HIGH)) / DAMPING
    return result, mul_nt(result, residual, HIGH)


def local_image(direction, hi_ref, lo_ref):
    rounded = direction.astype(BF16)
    return mul_nn(rounded, hi_ref[...]) + mul_nn(rounded, lo_ref[...])


def first_kernel(sel_ref, sketch_ref, e_ref, hi_ref, lo_ref, inv_ref, d_ref, gamma_ref, image_ref):
    sketch = sketch_ref[...]
    picked = jnp.where(selection(sel_ref, sketch.shape[1]), DAMPING, 0.0)
    neg_inv = negative_inverse(mul_nt(sketch, sketch + picked, HIGH))
    inv_ref[...] = neg_inv
    direction, gamma = precondition(e_ref[...], sketch, neg_inv)
    d_ref[...] = direction
    gamma_ref[...] = gamma
    image_ref[...] = local_image(direction, hi_ref, lo_ref)


def second_kernel(
    sum_ref, d_ref, e_ref, inv_ref, sketch_ref, gamma_ref, hi_ref, lo_ref, d1_ref, alpha_ref, gamma1_ref, curv_ref
):
    direction, gamma = d_ref[...], gamma_ref[...]
    image = sum_ref[...] + DAMPING * direction
    alpha = solve_small(mul_nt(direction, image, HIGH), gamma)
    alpha_ref[...] = alpha
    residual = e_ref[...] - mul_tn(alpha, image, HIGH)
    result, gamma1 = precondition(residual, sketch_ref[...], inv_ref[...])
    gamma1_ref[...] = gamma1
    direction1 = result + mul_tn(solve_small(gamma, gamma1), direction, HIGH)
    d1_ref[...] = direction1
    curvature = mul_nt(direction1, local_image(direction1, hi_ref, lo_ref), HIGH)
    nv = curvature.shape[0]
    flat = jnp.concatenate([curvature[i : i + 1, :] for i in range(nv)] + [jnp.zeros((1, 128 - nv * nv), F32)], axis=1)
    curv_ref[...] = jnp.broadcast_to(flat[None], curv_ref.shape)


def last_kernel(curv_ref, d_ref, d1_ref, alpha_ref, gamma1_ref, projected_ref, solution_ref, update_ref):
    d1, alpha = d1_ref[...], alpha_ref[...]
    nv = alpha.shape[0]
    flat = jnp.sum(curv_ref[...], axis=0)
    curvature = jnp.concatenate([flat[:, nv * i : nv * i + nv] for i in range(nv)])
    curvature = curvature + DAMPING * mul_nt(d1, d1, HIGH)
    alpha1 = solve_small(curvature, gamma1_ref[...])
    solution_ref[...] = mul_tn(alpha, d_ref[...], HIGH) + mul_tn(alpha1, d1, HIGH)
    update = mul_tn(jnp.concatenate([alpha, alpha1]), projected_ref[...], HIGH).astype(update_ref.dtype)
    for i in range(update_ref.shape[0]):
        update_ref[i] = update


def call(kernel, name, outs, *args):
    return pl.pallas_call(
        kernel,
        out_shape=[jax.ShapeDtypeStruct(shape, dtype) for shape, dtype in outs],
        compiler_params=pltpu.CompilerParams(vmem_limit_bytes=24 * 1024 * 1024),
        name=name,
    )(*args)


def body(log_derivs, energies, nys_rows):
    samp_rows, nv = energies.shape
    per_group = nys_rows.shape[1]
    groups = lax.axis_size(SAMP)
    n = samp_rows * groups
    rank = per_group * groups
    devices = lax.axis_size(EVERY)
    total_cols = log_derivs.shape[1] * lax.axis_size(PAR)

    cols = log_derivs.shape[1] // groups
    slab = lax.all_to_all(pack(log_derivs, groups, energies.T, nys_rows), SAMP, 0, 0, tiled=True)
    centered, pieces, e, selected = sketch_call(slab, cols, nv, per_group, 1.0 / math.sqrt(total_cols))
    high, low = gram(centered)

    got = lax.all_to_all(pieces, EVERY, 0, 0, tiled=True)
    got, high, low = lax.optimization_barrier((got, high, low))
    own = jnp.sum(got, axis=0)
    pieces = lax.all_to_all(jnp.broadcast_to(own[None], pieces.shape), EVERY, 0, 0, tiled=True)
    sketch = pieces.reshape(rank // 8, n // 128, 8, 128).swapaxes(1, 2).reshape(rank, n)

    vec, mat = ((nv, n), F32), ((nv, nv), F32)
    neg_inv, d0, gamma0, image = call(
        first_kernel, "first", [((rank, rank), F32), vec, mat, vec], selected, sketch, e, high, low
    )
    image = sum_everywhere(image)
    d1, alpha0, gamma1, curvature = call(
        second_kernel, "second", [vec, mat, mat, ((devices, 1, 128), F32)], image, d0, e, neg_inv, sketch, gamma0, high, low
    )
    curvature = lax.all_to_all(curvature, EVERY, 0, 0, tiled=True)
    (projected,) = call(project_kernel, "project", [((2 * nv, cols), F32)], d0, d1, centered)
    solution, update = call(
        last_kernel, "last", [vec, ((groups, nv, cols), BF16)], curvature, d0, d1, alpha0, gamma1, projected
    )
    blocks = lax.all_to_all(update, SAMP, 0, 0, tiled=True)
    update = jnp.moveaxis(blocks.astype(F32), 0, 1).reshape(nv, -1).T
    start = lax.axis_index(SAMP) * samp_rows
    return update, lax.dynamic_slice_in_dim(solution, start, samp_rows, 1).T


def solution(mesh):
    finer = Mesh(mesh.devices.reshape(4, 4, 4, 2), EVERY)
    in_specs = (P(SAMP, PAR), P(SAMP, None), P(SAMP, None))
    out_specs = (P(PAR, None), P(SAMP, None))
    return jax.shard_map(body, mesh=finer, in_specs=in_specs, out_specs=out_specs, check_vma=False)
```

```python
import functools
import math

import jax
import jax.numpy as jnp
from jax import lax
from jax.experimental import pallas as pl
from jax.experimental.pallas import tpu as pltpu
from jax.sharding import Mesh
from jax.sharding import PartitionSpec as P

DAMPING = 0.5
SAMP = ("y", "x")
PAR = ("z", "c")
EVERY = ("y", "x", "z", "c")
F32 = jnp.float32
BF16 = jnp.bfloat16
HIGH = lax.Precision.HIGHEST


def mul_nn(a, b, precision=None):
    return lax.dot_general(a, b, (((1,), (0,)), ((), ())), precision=precision, preferred_element_type=F32)


def mul_nt(a, b, precision=None):
    return lax.dot_general(a, b, (((1,), (1,)), ((), ())), precision=precision, preferred_element_type=F32)


def mul_tn(a, b, precision=None):
    return lax.dot_general(a, b, (((0,), (0,)), ((), ())), precision=precision, preferred_element_type=F32)


def shift(value, axis, by):
    n = lax.axis_size(axis)
    return lax.ppermute(value, axis, [(i, (i + by) % n) for i in range(n)])


def sum_axis(value, axis):
    n = lax.axis_size(axis)
    if n == 2:
        return value + shift(value, axis, 1)
    one, two, three = shift(value, axis, 1), shift(value, axis, 2), shift(value, axis, 3)
    return (value + two) + (one + three)


def sum_everywhere(value):
    for axis in ("c", "x", "y", "z"):
        value = sum_axis(value, axis)
    return value


def eliminate(cols, right, rows):
    b = len(cols)
    cols = list(cols)
    for j in range(b):
        col = cols[j]
        inv = 1.0 / col[j : j + 1, :]
        line = right[j : j + 1, :] * inv
        right = jnp.where(rows == j, line, right - col * line)
        for m in range(j + 1, b):
            line = cols[m][j : j + 1, :] * inv
            cols[m] = jnp.where(rows == j, line, cols[m] - col * line)
    return right


def solve_small(matrix, right):
    b = matrix.shape[0]
    rows = lax.broadcasted_iota(jnp.int32, right.shape, 0)
    cols = [jnp.broadcast_to(matrix[:, m : m + 1], right.shape) for m in range(b)]
    return eliminate(cols, right, rows)


def negative_inverse(a, b=16):
    n = a.shape[0]
    rows = lax.broadcasted_iota(jnp.int32, (b, n), 0)
    lanes = lax.broadcasted_iota(jnp.int32, (b, n), 1)
    all_rows = lax.broadcasted_iota(jnp.int32, (n, n), 0)
    all_lanes = lax.broadcasted_iota(jnp.int32, (n, n), 1)
    for k in range(0, n, b):
        panel = a[k : k + b, :]
        inside = (lanes >= k) & (lanes < k + b)
        left = jnp.where(inside, jnp.where(lanes == rows + k, 1.0, 0.0), panel)
        cols = [jnp.broadcast_to(panel[:, k + m : k + m + 1], (b, n)) for m in range(b)]
        right = eliminate(cols, left, rows)
        touched = ((all_rows >= k) & (all_rows < k + b)) | ((all_lanes >= k) & (all_lanes < k + b))
        a = jnp.where(touched, 0.0, a) - mul_tn(left, right, HIGH)
    return a


def pack_kernel(l_ref, e_in, picks_in, out_ref, e_ref, picks_ref, sems):
    parts, rows, width = out_ref.shape
    width -= 128
    loads = [
        pltpu.make_async_copy(
            l_ref.at[:, pl.ds(i * width, width)], out_ref.at[i, :, pl.ds(0, width)], sems.at[i]
        )
        for i in range(parts)
    ]
    small = [
        pltpu.make_async_copy(e_in, e_ref, sems.at[parts]),
        pltpu.make_async_copy(picks_in, picks_ref, sems.at[parts + 1]),
    ]
    for load in small + loads:
        load.start()
    for load in small:
        load.wait()
    e = e_ref[...]
    nv, group_rows = e.shape
    upper = e.astype(BF16).astype(F32)
    middle = (e - upper).astype(BF16).astype(F32)
    lower = e - upper - middle
    square = (picks_ref.shape[1],) * 2
    diagonal = lax.broadcasted_iota(jnp.int32, square, 0) == lax.broadcasted_iota(jnp.int32, square, 1)
    picks = jnp.broadcast_to(picks_ref[...].astype(F32), square)
    picks = jnp.sum(jnp.where(diagonal, picks, 0.0), axis=1, keepdims=True)
    side = (nv, 128 - group_rows)
    picks = jnp.where(lax.broadcasted_iota(jnp.int32, side, 1) == 0, picks, 0.0)
    none = jnp.zeros(side, F32)
    tile = jnp.concatenate(
        [
            jnp.concatenate([upper, picks], axis=1),
            jnp.concatenate([middle, none], axis=1),
            jnp.concatenate([lower, none], axis=1),
            jnp.zeros((rows - 3 * nv, 128), F32),
        ]
    ).astype(BF16)
    for i in range(parts):
        out_ref[i, :, width:] = tile
    for load in loads:
        load.wait()


def pack(local, parts, energies, picks):
    rows, cols = local.shape[0], local.shape[1] // parts
    vmem = pl.BlockSpec(memory_space=pltpu.VMEM)
    return pl.pallas_call(
        pack_kernel,
        in_specs=[pl.BlockSpec(memory_space=pl.ANY)] * 3,
        out_specs=vmem,
        out_shape=jax.ShapeDtypeStruct((parts, rows, cols + 128), BF16),
        scratch_shapes=[
            pltpu.VMEM(energies.shape, F32),
            pltpu.VMEM(picks.shape, jnp.int32),
            pltpu.SemaphoreType.DMA((parts + 2,)),
        ],
        compiler_params=pltpu.CompilerParams(vmem_limit_bytes=48 * 1024 * 1024),
        name="pack",
    )(local, energies, picks)


def selection(sel_ref, n):
    return lax.broadcasted_iota(jnp.int32, (sel_ref.shape[0], n), 1) == sel_ref[...]


def sketch_kernel(scale, slab_ref, c_ref, sketch_ref, e_ref, sel_ref, pick_ref, acc_ref):
    groups, rows, _ = slab_ref.shape
    n, cols = c_ref.shape
    nv = e_ref.shape[0]
    for i in range(groups):
        tile = slab_ref[i, 0:32, cols:].astype(F32)
        upper, middle, lower = tile[0:nv], tile[nv : 2 * nv], tile[2 * nv : 3 * nv]
        e_ref[:, i * rows : (i + 1) * rows] = (upper + (middle + lower))[:, :rows]
        sel_ref[i * nv : (i + 1) * nv, :] = upper[:, rows : rows + 1].astype(jnp.int32) + i * rows
    pick_ref[...] = jnp.where(selection(sel_ref, n), 1.0, 0.0).astype(BF16)
    width = min(512, cols)
    for start in range(0, cols, width):
        place = slice(start, start + width)
        total = 0.0
        for i in range(groups):
            total = total + jnp.sum(slab_ref[i, :, place].astype(F32), axis=0, keepdims=True)
        mean = total / n
        for i in range(groups):
            c_ref[i * rows : (i + 1) * rows, place] = ((slab_ref[i, :, place].astype(F32) - mean) * scale).astype(BF16)
        chosen = mul_nn(pick_ref[...], c_ref[:, place]).astype(BF16)
        product = mul_nt(chosen, c_ref[:, place])
        acc_ref[...] = product if start == 0 else acc_ref[...] + product
    for i in range(0, acc_ref.shape[0], 8):
        for j in range(0, n, 128):
            sketch_ref[i * n // 1024 + j // 128] = acc_ref[i : i + 8, j : j + 128]


def sketch_call(slab, cols, nv, per_group, scale):
    groups, rows, _ = slab.shape
    rank, n = per_group * groups, groups * rows
    return pl.pallas_call(
        functools.partial(sketch_kernel, scale),
        in_specs=[pl.BlockSpec(memory_space=pltpu.VMEM)],
        out_specs=[pl.BlockSpec(memory_space=pltpu.VMEM)] * 4,
        out_shape=[
            jax.ShapeDtypeStruct((n, cols), BF16),
            jax.ShapeDtypeStruct((rank * n // 1024, 8, 128), F32),
            jax.ShapeDtypeStruct((nv, n), F32),
            jax.ShapeDtypeStruct((rank, 1), jnp.int32),
        ],
        scratch_shapes=[pltpu.VMEM((rank, n), BF16), pltpu.VMEM((rank, n), F32)],
        compiler_params=pltpu.CompilerParams(vmem_limit_bytes=24 * 1024 * 1024),
        name="sketch",
    )(slab)


def precondition(residual, sketch, neg_inv):
    coeffs = mul_nn(mul_nt(residual, sketch, HIGH), neg_inv, HIGH)
    result = (residual + mul_nn(coeffs, sketch, HIGH)) / DAMPING
    return result, mul_nt(result, residual, HIGH)


def three_parts(value):
    upper = value.astype(BF16).astype(F32)
    middle = (value - upper).astype(BF16).astype(F32)
    return jnp.concatenate([upper, middle, value - upper - middle]).astype(BF16)


def first_kernel(sel_ref, sketch_ref, e_ref, c_ref, inv_ref, d_ref, gamma_ref, image_ref, projected_ref):
    sketch = sketch_ref[...]
    picked = jnp.where(selection(sel_ref, sketch.shape[1]), DAMPING, 0.0)
    neg_inv = negative_inverse(mul_nt(sketch, sketch + picked, HIGH))
    inv_ref[...] = neg_inv
    direction, gamma = precondition(e_ref[...], sketch, neg_inv)
    d_ref[...] = direction
    gamma_ref[...] = gamma
    projected = mul_nn(direction.astype(BF16), c_ref[...])
    projected_ref[...] = projected
    nv = direction.shape[0]
    image = mul_nt(three_parts(projected), c_ref[...])
    image_ref[...] = image[:nv] + (image[nv : 2 * nv] + image[2 * nv :])


def second_kernel(
    sum_ref, d_ref, e_ref, inv_ref, sketch_ref, gamma_ref, c_ref, d1_ref, alpha_ref, gamma1_ref, curv_ref, projected_ref
):
    direction, gamma = d_ref[...], gamma_ref[...]
    image = sum_ref[...] + DAMPING * direction
    alpha = solve_small(mul_nt(direction, image, HIGH), gamma)
    alpha_ref[...] = alpha
    residual = e_ref[...] - mul_tn(alpha, image, HIGH)
    result, gamma1 = precondition(residual, sketch_ref[...], inv_ref[...])
    gamma1_ref[...] = gamma1
    direction1 = result + mul_tn(solve_small(gamma, gamma1), direction, HIGH)
    d1_ref[...] = direction1
    nv = direction1.shape[0]
    parts = mul_nn(three_parts(direction1), c_ref[...])
    projected_ref[...] = parts[:nv]
    curvature = mul_nt(parts[:nv] + (parts[nv : 2 * nv] + parts[2 * nv :]), parts[:nv], HIGH)
    flat = jnp.concatenate([curvature[i : i + 1, :] for i in range(nv)] + [jnp.zeros((1, 128 - nv * nv), F32)], axis=1)
    curv_ref[...] = jnp.broadcast_to(flat[None], curv_ref.shape)


def last_kernel(curv_ref, d_ref, d1_ref, alpha_ref, gamma1_ref, p0_ref, p1_ref, solution_ref, update_ref):
    d1, alpha = d1_ref[...], alpha_ref[...]
    nv = alpha.shape[0]
    flat = jnp.sum(curv_ref[...], axis=0)
    curvature = jnp.concatenate([flat[:, nv * i : nv * i + nv] for i in range(nv)])
    curvature = curvature + DAMPING * mul_nt(d1, d1, HIGH)
    alpha1 = solve_small(curvature, gamma1_ref[...])
    solution_ref[...] = mul_tn(alpha, d_ref[...], HIGH) + mul_tn(alpha1, d1, HIGH)
    both = jnp.concatenate([p0_ref[...], p1_ref[...]])
    update = mul_tn(jnp.concatenate([alpha, alpha1]), both, HIGH).astype(update_ref.dtype)
    for i in range(update_ref.shape[0]):
        update_ref[i] = update


def call(kernel, name, outs, *args):
    return pl.pallas_call(
        kernel,
        out_shape=[jax.ShapeDtypeStruct(shape, dtype) for shape, dtype in outs],
        compiler_params=pltpu.CompilerParams(vmem_limit_bytes=24 * 1024 * 1024),
        name=name,
    )(*args)


def body(log_derivs, energies, nys_rows):
    samp_rows, nv = energies.shape
    per_group = nys_rows.shape[1]
    groups = lax.axis_size(SAMP)
    n = samp_rows * groups
    rank = per_group * groups
    devices = lax.axis_size(EVERY)
    total_cols = log_derivs.shape[1] * lax.axis_size(PAR)

    cols = log_derivs.shape[1] // groups
    slab = lax.all_to_all(pack(log_derivs, groups, energies.T, nys_rows), SAMP, 0, 0, tiled=True)
    centered, pieces, e, selected = sketch_call(slab, cols, nv, per_group, 1.0 / math.sqrt(total_cols))
    got = lax.all_to_all(pieces, EVERY, 0, 0, tiled=True)
    own = jnp.sum(got, axis=0)
    pieces = lax.all_to_all(jnp.broadcast_to(own[None], pieces.shape), EVERY, 0, 0, tiled=True)
    sketch = pieces.reshape(rank // 8, n // 128, 8, 128).swapaxes(1, 2).reshape(rank, n)

    vec, mat = ((nv, n), F32), ((nv, nv), F32)
    projected = ((nv, cols), F32)
    neg_inv, d0, gamma0, image, p0 = call(
        first_kernel, "first", [((rank, rank), F32), vec, mat, vec, projected], selected, sketch, e, centered
    )
    image = sum_everywhere(image)
    d1, alpha0, gamma1, curvature, p1 = call(
        second_kernel,
        "second",
        [vec, mat, mat, ((devices, 1, 128), F32), projected],
        image,
        d0,
        e,
        neg_inv,
        sketch,
        gamma0,
        centered,
    )
    curvature = lax.all_to_all(curvature, EVERY, 0, 0, tiled=True)
    solution, update = call(
        last_kernel, "last", [vec, ((groups, nv, cols), BF16)], curvature, d0, d1, alpha0, gamma1, p0, p1
    )
    start = lax.axis_index(SAMP) * samp_rows
    own = lax.dynamic_slice_in_dim(solution, start, samp_rows, 1).T
    update, own = lax.optimization_barrier((update, own))
    blocks = lax.all_to_all(update, SAMP, 0, 0, tiled=True)
    update = jnp.moveaxis(blocks.astype(F32), 0, 1).reshape(nv, -1).T
    return update, own


def solution(mesh):
    finer = Mesh(mesh.devices.reshape(4, 4, 4, 2), EVERY)
    in_specs = (P(SAMP, PAR), P(SAMP, None), P(SAMP, None))
    out_specs = (P(PAR, None), P(SAMP, None))
    return jax.shard_map(body, mesh=finer, in_specs=in_specs, out_specs=out_specs, check_vma=False)
```

```python
import functools
import math

import jax
import jax.numpy as jnp
from jax import lax
from jax.experimental import pallas as pl
from jax.experimental.pallas import tpu as pltpu
from jax.sharding import Mesh
from jax.sharding import PartitionSpec as P

DAMPING = 0.5
SAMP = ("y", "x")
PAR = ("z", "c")
EVERY = ("y", "x", "z", "c")
F32 = jnp.float32
BF16 = jnp.bfloat16
HIGH = lax.Precision.HIGHEST


def mul_nn(a, b, precision=None):
    return lax.dot_general(a, b, (((1,), (0,)), ((), ())), precision=precision, preferred_element_type=F32)


def mul_nt(a, b, precision=None):
    return lax.dot_general(a, b, (((1,), (1,)), ((), ())), precision=precision, preferred_element_type=F32)


def mul_tn(a, b, precision=None):
    return lax.dot_general(a, b, (((0,), (0,)), ((), ())), precision=precision, preferred_element_type=F32)


def shift(value, axis, by):
    n = lax.axis_size(axis)
    return lax.ppermute(value, axis, [(i, (i + by) % n) for i in range(n)])


def sum_axis(value, axis):
    n = lax.axis_size(axis)
    if n == 2:
        return value + shift(value, axis, 1)
    one, two, three = shift(value, axis, 1), shift(value, axis, 2), shift(value, axis, 3)
    return (value + two) + (one + three)


def sum_everywhere(value):
    for axis in ("c", "x", "y", "z"):
        value = sum_axis(value, axis)
    return value


def eliminate(cols, right, rows):
    b = len(cols)
    cols = list(cols)
    for j in range(b):
        col = cols[j]
        inv = 1.0 / col[j : j + 1, :]
        line = right[j : j + 1, :] * inv
        right = jnp.where(rows == j, line, right - col * line)
        for m in range(j + 1, b):
            line = cols[m][j : j + 1, :] * inv
            cols[m] = jnp.where(rows == j, line, cols[m] - col * line)
    return right


def solve_small(matrix, right):
    b = matrix.shape[0]
    rows = lax.broadcasted_iota(jnp.int32, right.shape, 0)
    cols = [jnp.broadcast_to(matrix[:, m : m + 1], right.shape) for m in range(b)]
    return eliminate(cols, right, rows)


def negative_inverse(a, b=16):
    n = a.shape[0]
    rows = lax.broadcasted_iota(jnp.int32, (b, n), 0)
    lanes = lax.broadcasted_iota(jnp.int32, (b, n), 1)
    all_rows = lax.broadcasted_iota(jnp.int32, (n, n), 0)
    all_lanes = lax.broadcasted_iota(jnp.int32, (n, n), 1)
    for k in range(0, n, b):
        panel = a[k : k + b, :]
        inside = (lanes >= k) & (lanes < k + b)
        left = jnp.where(inside, jnp.where(lanes == rows + k, 1.0, 0.0), panel)
        cols = [jnp.broadcast_to(panel[:, k + m : k + m + 1], (b, n)) for m in range(b)]
        right = eliminate(cols, left, rows)
        touched = ((all_rows >= k) & (all_rows < k + b)) | ((all_lanes >= k) & (all_lanes < k + b))
        a = jnp.where(touched, 0.0, a) - mul_tn(left, right, HIGH)
    return a


def pack_kernel(l_ref, e_in, picks_in, out_ref, e_ref, picks_ref, sems):
    parts, rows, width = out_ref.shape
    width -= 128
    loads = [
        pltpu.make_async_copy(
            l_ref.at[:, pl.ds(i * width, width)], out_ref.at[i, :, pl.ds(0, width)], sems.at[i]
        )
        for i in range(parts)
    ]
    small = [
        pltpu.make_async_copy(e_in, e_ref, sems.at[parts]),
        pltpu.make_async_copy(picks_in, picks_ref, sems.at[parts + 1]),
    ]
    for load in small + loads:
        load.start()
    for load in small:
        load.wait()
    e = e_ref[...]
    nv, group_rows = e.shape
    upper = e.astype(BF16).astype(F32)
    middle = (e - upper).astype(BF16).astype(F32)
    lower = e - upper - middle
    square = (picks_ref.shape[1],) * 2
    diagonal = lax.broadcasted_iota(jnp.int32, square, 0) == lax.broadcasted_iota(jnp.int32, square, 1)
    picks = jnp.broadcast_to(picks_ref[...].astype(F32), square)
    picks = jnp.sum(jnp.where(diagonal, picks, 0.0), axis=1, keepdims=True)
    side = (nv, 128 - group_rows)
    picks = jnp.where(lax.broadcasted_iota(jnp.int32, side, 1) == 0, picks, 0.0)
    none = jnp.zeros(side, F32)
    tile = jnp.concatenate(
        [
            jnp.concatenate([upper, picks], axis=1),
            jnp.concatenate([middle, none], axis=1),
            jnp.concatenate([lower, none], axis=1),
            jnp.zeros((rows - 3 * nv, 128), F32),
        ]
    ).astype(BF16)
    for i in range(parts):
        out_ref[i, :, width:] = tile
    for load in loads:
        load.wait()


def pack(local, parts, energies, picks):
    rows, cols = local.shape[0], local.shape[1] // parts
    vmem = pl.BlockSpec(memory_space=pltpu.VMEM)
    return pl.pallas_call(
        pack_kernel,
        in_specs=[pl.BlockSpec(memory_space=pl.ANY)] * 3,
        out_specs=vmem,
        out_shape=jax.ShapeDtypeStruct((parts, rows, cols + 128), BF16),
        scratch_shapes=[
            pltpu.VMEM(energies.shape, F32),
            pltpu.VMEM(picks.shape, jnp.int32),
            pltpu.SemaphoreType.DMA((parts + 2,)),
        ],
        compiler_params=pltpu.CompilerParams(vmem_limit_bytes=48 * 1024 * 1024),
        name="pack",
    )(local, energies, picks)


def selection(sel_ref, n):
    return lax.broadcasted_iota(jnp.int32, (sel_ref.shape[0], n), 1) == sel_ref[...]


def sketch_kernel(
    scale, slab_in, c_out, sketch_ref, e_ref, sel_ref, slab_ref, c_ref, pick_ref, acc_ref, sems, load_sems
):
    groups, rows, _ = slab_ref.shape
    cols = c_out.shape[1]
    width = min(512, cols)
    windows = [(cols, 128)] + [(start, width) for start in range(0, cols, width)]
    loads = [
        pltpu.make_async_copy(
            slab_in.at[:, :, pl.ds(start, size)], slab_ref.at[:, :, pl.ds(start, size)], load_sems.at[i]
        )
        for i, (start, size) in enumerate(windows)
    ]
    for load in loads:
        load.start()
    loads.pop(0).wait()
    n = groups * rows
    nv = e_ref.shape[0]
    for i in range(groups):
        tile = slab_ref[i, 0:32, cols:].astype(F32)
        upper, middle, lower = tile[0:nv], tile[nv : 2 * nv], tile[2 * nv : 3 * nv]
        e_ref[:, i * rows : (i + 1) * rows] = (upper + (middle + lower))[:, :rows]
        sel_ref[i * nv : (i + 1) * nv, :] = upper[:, rows : rows + 1].astype(jnp.int32) + i * rows
    pick_ref[...] = jnp.where(selection(sel_ref, n), 1.0, 0.0).astype(BF16)
    stores = []
    for start in range(0, cols, width):
        place = slice(start, start + width)
        loads[start // width].wait()
        total = 0.0
        for i in range(groups):
            total = total + jnp.sum(slab_ref[i, :, place].astype(F32), axis=0, keepdims=True)
        mean = total / n
        for i in range(groups):
            c_ref[i * rows : (i + 1) * rows, place] = ((slab_ref[i, :, place].astype(F32) - mean) * scale).astype(BF16)
        window = pl.ds(start, width)
        stores.append(
            pltpu.make_async_copy(c_ref.at[:, window], c_out.at[:, window], sems.at[start // width])
        )
        stores[-1].start()
        chosen = mul_nn(pick_ref[...], c_ref[:, place]).astype(BF16)
        product = mul_nt(chosen, c_ref[:, place])
        acc_ref[...] = product if start == 0 else acc_ref[...] + product
    for i in range(0, acc_ref.shape[0], 8):
        for j in range(0, n, 128):
            sketch_ref[i * n // 1024 + j // 128] = acc_ref[i : i + 8, j : j + 128]
    for store in stores:
        store.wait()


def sketch_call(slab, cols, nv, per_group, scale):
    groups, rows, _ = slab.shape
    rank, n = per_group * groups, groups * rows
    return pl.pallas_call(
        functools.partial(sketch_kernel, scale),
        in_specs=[pl.BlockSpec(memory_space=pl.ANY)],
        out_specs=[pl.BlockSpec(memory_space=pl.ANY)] + [pl.BlockSpec(memory_space=pltpu.VMEM)] * 3,
        out_shape=[
            jax.ShapeDtypeStruct((n, cols), BF16),
            jax.ShapeDtypeStruct((rank * n // 1024, 8, 128), F32),
            jax.ShapeDtypeStruct((nv, n), F32),
            jax.ShapeDtypeStruct((rank, 1), jnp.int32),
        ],
        scratch_shapes=[
            pltpu.VMEM(slab.shape, BF16),
            pltpu.VMEM((n, cols), BF16),
            pltpu.VMEM((rank, n), BF16),
            pltpu.VMEM((rank, n), F32),
            pltpu.SemaphoreType.DMA((-(-cols // 512),)),
            pltpu.SemaphoreType.DMA((-(-cols // 512) + 1,)),
        ],
        compiler_params=pltpu.CompilerParams(vmem_limit_bytes=46 * 1024 * 1024),
        name="sketch",
    )(slab)


def precondition(residual, sketch, neg_inv):
    coeffs = mul_nn(mul_nt(residual, sketch, HIGH), neg_inv, HIGH)
    result = (residual + mul_nn(coeffs, sketch, HIGH)) / DAMPING
    return result, mul_nt(result, residual, HIGH)


def three_parts(value):
    upper = value.astype(BF16).astype(F32)
    middle = (value - upper).astype(BF16).astype(F32)
    return jnp.concatenate([upper, middle, value - upper - middle]).astype(BF16)


def first_kernel(
    sel_ref, sketch_ref, e_ref, c_in, inv_ref, d_ref, gamma_ref, image_ref, projected_ref, c_ref, sem
):
    load = pltpu.make_async_copy(c_in, c_ref, sem.at[0])
    load.start()
    sketch = sketch_ref[...]
    picked = jnp.where(selection(sel_ref, sketch.shape[1]), DAMPING, 0.0)
    neg_inv = negative_inverse(mul_nt(sketch, sketch + picked, HIGH))
    inv_ref[...] = neg_inv
    direction, gamma = precondition(e_ref[...], sketch, neg_inv)
    d_ref[...] = direction
    gamma_ref[...] = gamma
    load.wait()
    projected = mul_nn(direction.astype(BF16), c_ref[...])
    projected_ref[...] = projected
    nv = direction.shape[0]
    image = mul_nt(three_parts(projected), c_ref[...])
    image_ref[...] = image[:nv] + (image[nv : 2 * nv] + image[2 * nv :])


def second_kernel(
    sum_ref,
    d_ref,
    e_ref,
    inv_ref,
    sketch_ref,
    gamma_ref,
    c_in,
    d1_ref,
    alpha_ref,
    gamma1_ref,
    curv_ref,
    projected_ref,
    c_ref,
    sem,
):
    load = pltpu.make_async_copy(c_in, c_ref, sem.at[0])
    load.start()
    direction, gamma = d_ref[...], gamma_ref[...]
    image = sum_ref[...] + DAMPING * direction
    alpha = solve_small(mul_nt(direction, image, HIGH), gamma)
    alpha_ref[...] = alpha
    residual = e_ref[...] - mul_tn(alpha, image, HIGH)
    result, gamma1 = precondition(residual, sketch_ref[...], inv_ref[...])
    gamma1_ref[...] = gamma1
    direction1 = result + mul_tn(solve_small(gamma, gamma1), direction, HIGH)
    d1_ref[...] = direction1
    nv = direction1.shape[0]
    load.wait()
    parts = mul_nn(three_parts(direction1), c_ref[...])
    projected_ref[...] = parts[:nv]
    curvature = mul_nt(parts[:nv] + (parts[nv : 2 * nv] + parts[2 * nv :]), parts[:nv], HIGH)
    flat = jnp.concatenate([curvature[i : i + 1, :] for i in range(nv)] + [jnp.zeros((1, 128 - nv * nv), F32)], axis=1)
    curv_ref[...] = jnp.broadcast_to(flat[None], curv_ref.shape)


def last_kernel(curv_ref, d_ref, d1_ref, alpha_ref, gamma1_ref, p0_ref, p1_ref, solution_ref, update_ref):
    d1, alpha = d1_ref[...], alpha_ref[...]
    nv = alpha.shape[0]
    flat = jnp.sum(curv_ref[...], axis=0)
    curvature = jnp.concatenate([flat[:, nv * i : nv * i + nv] for i in range(nv)])
    curvature = curvature + DAMPING * mul_nt(d1, d1, HIGH)
    alpha1 = solve_small(curvature, gamma1_ref[...])
    solution_ref[...] = mul_tn(alpha, d_ref[...], HIGH) + mul_tn(alpha1, d1, HIGH)
    both = jnp.concatenate([p0_ref[...], p1_ref[...]])
    update = mul_tn(jnp.concatenate([alpha, alpha1]), both, HIGH).astype(update_ref.dtype)
    for i in range(update_ref.shape[0]):
        update_ref[i] = update


def call(kernel, name, outs, *args, slab=None):
    vmem = pl.BlockSpec(memory_space=pltpu.VMEM)
    held = [] if slab is None else [slab]
    return pl.pallas_call(
        kernel,
        in_specs=[vmem] * len(args) + [pl.BlockSpec(memory_space=pl.ANY)] * len(held),
        out_specs=[vmem] * len(outs),
        out_shape=[jax.ShapeDtypeStruct(shape, dtype) for shape, dtype in outs],
        scratch_shapes=[scratch for x in held for scratch in (pltpu.VMEM(x.shape, x.dtype), pltpu.SemaphoreType.DMA((1,)))],
        compiler_params=pltpu.CompilerParams(vmem_limit_bytes=(46 if held else 24) * 1024 * 1024),
        name=name,
    )(*args, *held)


def body(log_derivs, energies, nys_rows):
    samp_rows, nv = energies.shape
    per_group = nys_rows.shape[1]
    groups = lax.axis_size(SAMP)
    n = samp_rows * groups
    rank = per_group * groups
    devices = lax.axis_size(EVERY)
    total_cols = log_derivs.shape[1] * lax.axis_size(PAR)

    cols = log_derivs.shape[1] // groups
    slab = lax.all_to_all(pack(log_derivs, groups, energies.T, nys_rows), SAMP, 0, 0, tiled=True)
    centered, pieces, e, selected = sketch_call(slab, cols, nv, per_group, 1.0 / math.sqrt(total_cols))
    got = lax.all_to_all(pieces, EVERY, 0, 0, tiled=True)
    own = jnp.sum(got, axis=0)
    pieces = lax.all_to_all(jnp.broadcast_to(own[None], pieces.shape), EVERY, 0, 0, tiled=True)
    sketch = pieces.reshape(rank // 8, n // 128, 8, 128).swapaxes(1, 2).reshape(rank, n)

    vec, mat = ((nv, n), F32), ((nv, nv), F32)
    projected = ((nv, cols), F32)
    neg_inv, d0, gamma0, image, p0 = call(
        first_kernel, "first", [((rank, rank), F32), vec, mat, vec, projected], selected, sketch, e, slab=centered
    )
    image = sum_everywhere(image)
    d1, alpha0, gamma1, curvature, p1 = call(
        second_kernel,
        "second",
        [vec, mat, mat, ((devices, 1, 128), F32), projected],
        image,
        d0,
        e,
        neg_inv,
        sketch,
        gamma0,
        slab=centered,
    )
    start = (lax.axis_index(SAMP) * samp_rows).astype(jnp.uint32)
    curvature, start = lax.optimization_barrier((curvature, start))
    curvature = lax.all_to_all(curvature, EVERY, 0, 0, tiled=True)
    solution, update = call(
        last_kernel, "last", [vec, ((groups, nv, cols), BF16)], curvature, d0, d1, alpha0, gamma1, p0, p1
    )
    own = lax.dynamic_slice(solution, (jnp.uint32(0), start), (nv, samp_rows)).T
    update, own = lax.optimization_barrier((update, own))
    blocks = lax.all_to_all(update, SAMP, 0, 0, tiled=True)
    update = jnp.moveaxis(blocks.astype(F32), 0, 1).reshape(nv, -1).T
    return update, own


def solution(mesh):
    finer = Mesh(mesh.devices.reshape(4, 4, 4, 2), EVERY)
    in_specs = (P(SAMP, PAR), P(SAMP, None), P(SAMP, None))
    out_specs = (P(PAR, None), P(SAMP, None))
    return jax.shard_map(body, mesh=finer, in_specs=in_specs, out_specs=out_specs, check_vma=False)
```

```python
import functools
import math

import jax
import jax.numpy as jnp
from jax import lax
from jax.experimental import pallas as pl
from jax.experimental.pallas import tpu as pltpu
from jax.sharding import Mesh
from jax.sharding import PartitionSpec as P

DAMPING = 0.5
SAMP = ("y", "x")
PAR = ("z", "c")
EVERY = ("y", "x", "z", "c")
F32 = jnp.float32
BF16 = jnp.bfloat16
HIGH = lax.Precision.HIGHEST


def mul_nn(a, b, precision=None):
    return lax.dot_general(a, b, (((1,), (0,)), ((), ())), precision=precision, preferred_element_type=F32)


def mul_nt(a, b, precision=None):
    return lax.dot_general(a, b, (((1,), (1,)), ((), ())), precision=precision, preferred_element_type=F32)


def mul_tn(a, b, precision=None):
    return lax.dot_general(a, b, (((0,), (0,)), ((), ())), precision=precision, preferred_element_type=F32)


def shift(value, axis, by):
    n = lax.axis_size(axis)
    return lax.ppermute(value, axis, [(i, (i + by) % n) for i in range(n)])


def sum_axis(value, axis):
    n = lax.axis_size(axis)
    if n == 2:
        return value + shift(value, axis, 1)
    one, two, three = shift(value, axis, 1), shift(value, axis, 2), shift(value, axis, 3)
    return (value + two) + (one + three)


def sum_everywhere(value):
    for axis in ("c", "x", "y", "z"):
        value = sum_axis(value, axis)
    return value


def eliminate(cols, right, rows):
    b = len(cols)
    cols = list(cols)
    for j in range(b):
        col = cols[j]
        inv = 1.0 / col[j : j + 1, :]
        line = right[j : j + 1, :] * inv
        right = jnp.where(rows == j, line, right - col * line)
        for m in range(j + 1, b):
            line = cols[m][j : j + 1, :] * inv
            cols[m] = jnp.where(rows == j, line, cols[m] - col * line)
    return right


def solve_small(matrix, right):
    b = matrix.shape[0]
    rows = lax.broadcasted_iota(jnp.int32, right.shape, 0)
    cols = [jnp.broadcast_to(matrix[:, m : m + 1], right.shape) for m in range(b)]
    return eliminate(cols, right, rows)


def negative_inverse(a, b=16):
    n = a.shape[0]
    rows = lax.broadcasted_iota(jnp.int32, (b, n), 0)
    lanes = lax.broadcasted_iota(jnp.int32, (b, n), 1)
    all_rows = lax.broadcasted_iota(jnp.int32, (n, n), 0)
    all_lanes = lax.broadcasted_iota(jnp.int32, (n, n), 1)
    for k in range(0, n, b):
        panel = a[k : k + b, :]
        inside = (lanes >= k) & (lanes < k + b)
        left = jnp.where(inside, jnp.where(lanes == rows + k, 1.0, 0.0), panel)
        cols = [jnp.broadcast_to(panel[:, k + m : k + m + 1], (b, n)) for m in range(b)]
        right = eliminate(cols, left, rows)
        touched = ((all_rows >= k) & (all_rows < k + b)) | ((all_lanes >= k) & (all_lanes < k + b))
        a = jnp.where(touched, 0.0, a) - mul_tn(left, right, HIGH)
    return a


def pack_kernel(l_ref, e_in, picks_in, out_ref, e_ref, picks_ref, sems):
    parts, rows, width = out_ref.shape
    width -= 128
    loads = [
        pltpu.make_async_copy(
            l_ref.at[:, pl.ds(i * width, width)], out_ref.at[i, :, pl.ds(0, width)], sems.at[i]
        )
        for i in range(parts)
    ]
    small = [
        pltpu.make_async_copy(e_in, e_ref, sems.at[parts]),
        pltpu.make_async_copy(picks_in, picks_ref, sems.at[parts + 1]),
    ]
    for load in small + loads:
        load.start()
    for load in small:
        load.wait()
    e = e_ref[...]
    nv, group_rows = e.shape
    upper = e.astype(BF16).astype(F32)
    middle = (e - upper).astype(BF16).astype(F32)
    lower = e - upper - middle
    square = (picks_ref.shape[1],) * 2
    diagonal = lax.broadcasted_iota(jnp.int32, square, 0) == lax.broadcasted_iota(jnp.int32, square, 1)
    picks = jnp.broadcast_to(picks_ref[...].astype(F32), square)
    picks = jnp.sum(jnp.where(diagonal, picks, 0.0), axis=1, keepdims=True)
    side = (nv, 128 - group_rows)
    picks = jnp.where(lax.broadcasted_iota(jnp.int32, side, 1) == 0, picks, 0.0)
    none = jnp.zeros(side, F32)
    tile = jnp.concatenate(
        [
            jnp.concatenate([upper, picks], axis=1),
            jnp.concatenate([middle, none], axis=1),
            jnp.concatenate([lower, none], axis=1),
            jnp.zeros((rows - 3 * nv, 128), F32),
        ]
    ).astype(BF16)
    for i in range(parts):
        out_ref[i, :, width:] = tile
    for load in loads:
        load.wait()


def pack(local, parts, energies, picks):
    rows, cols = local.shape[0], local.shape[1] // parts
    vmem = pl.BlockSpec(memory_space=pltpu.VMEM)
    return pl.pallas_call(
        pack_kernel,
        in_specs=[pl.BlockSpec(memory_space=pl.ANY)] * 3,
        out_specs=vmem,
        out_shape=jax.ShapeDtypeStruct((parts, rows, cols + 128), BF16),
        scratch_shapes=[
            pltpu.VMEM(energies.shape, F32),
            pltpu.VMEM(picks.shape, jnp.int32),
            pltpu.SemaphoreType.DMA((parts + 2,)),
        ],
        compiler_params=pltpu.CompilerParams(vmem_limit_bytes=48 * 1024 * 1024),
        name="pack",
    )(local, energies, picks)


def selection(sel_ref, n):
    return lax.broadcasted_iota(jnp.int32, (sel_ref.shape[0], n), 1) == sel_ref[...]


def sketch_kernel(
    scale, slab_in, c_out, sketch_ref, e_ref, sel_ref, slab_ref, c_ref, pick_ref, acc_ref, sems, load_sems
):
    groups, rows, _ = slab_ref.shape
    cols = c_out.shape[1]
    width = min(512, cols)
    windows = [(cols, 128)] + [(start, width) for start in range(0, cols, width)]
    loads = [
        pltpu.make_async_copy(
            slab_in.at[:, :, pl.ds(start, size)], slab_ref.at[:, :, pl.ds(start, size)], load_sems.at[i]
        )
        for i, (start, size) in enumerate(windows)
    ]
    for load in loads:
        load.start()
    loads.pop(0).wait()
    n = groups * rows
    nv = e_ref.shape[0]
    for i in range(groups):
        tile = slab_ref[i, 0:32, cols:].astype(F32)
        upper, middle, lower = tile[0:nv], tile[nv : 2 * nv], tile[2 * nv : 3 * nv]
        e_ref[:, i * rows : (i + 1) * rows] = (upper + (middle + lower))[:, :rows]
        sel_ref[i * nv : (i + 1) * nv, :] = upper[:, rows : rows + 1].astype(jnp.int32) + i * rows
    pick_ref[...] = jnp.where(selection(sel_ref, n), 1.0, 0.0).astype(BF16)
    stores = []
    for start in range(0, cols, width):
        place = slice(start, start + width)
        loads[start // width].wait()
        total = 0.0
        for i in range(groups):
            total = total + jnp.sum(slab_ref[i, :, place].astype(F32), axis=0, keepdims=True)
        mean = total / n
        for i in range(groups):
            c_ref[i * rows : (i + 1) * rows, place] = ((slab_ref[i, :, place].astype(F32) - mean) * scale).astype(BF16)
        window = pl.ds(start, width)
        stores.append(
            pltpu.make_async_copy(c_ref.at[:, window], c_out.at[:, window], sems.at[start // width])
        )
        stores[-1].start()
        chosen = mul_nn(pick_ref[...], c_ref[:, place]).astype(BF16)
        product = mul_nt(chosen, c_ref[:, place])
        acc_ref[...] = product if start == 0 else acc_ref[...] + product
    for i in range(0, acc_ref.shape[0], 8):
        for j in range(0, n, 128):
            sketch_ref[i * n // 1024 + j // 128] = acc_ref[i : i + 8, j : j + 128]
    for store in stores:
        store.wait()


def sketch_call(slab, cols, nv, per_group, scale):
    groups, rows, _ = slab.shape
    rank, n = per_group * groups, groups * rows
    return pl.pallas_call(
        functools.partial(sketch_kernel, scale),
        in_specs=[pl.BlockSpec(memory_space=pl.ANY)],
        out_specs=[pl.BlockSpec(memory_space=pl.ANY)] + [pl.BlockSpec(memory_space=pltpu.VMEM)] * 3,
        out_shape=[
            jax.ShapeDtypeStruct((n, cols), BF16),
            jax.ShapeDtypeStruct((rank * n // 1024, 8, 128), F32),
            jax.ShapeDtypeStruct((nv, n), F32),
            jax.ShapeDtypeStruct((rank, 1), jnp.int32),
        ],
        scratch_shapes=[
            pltpu.VMEM(slab.shape, BF16),
            pltpu.VMEM((n, cols), BF16),
            pltpu.VMEM((rank, n), BF16),
            pltpu.VMEM((rank, n), F32),
            pltpu.SemaphoreType.DMA((-(-cols // 512),)),
            pltpu.SemaphoreType.DMA((-(-cols // 512) + 1,)),
        ],
        compiler_params=pltpu.CompilerParams(vmem_limit_bytes=46 * 1024 * 1024),
        name="sketch",
    )(slab)


def precondition(residual, sketch, neg_inv):
    coeffs = mul_nn(mul_nt(residual, sketch, HIGH), neg_inv, HIGH)
    result = (residual + mul_nn(coeffs, sketch, HIGH)) / DAMPING
    return result, mul_nt(result, residual, HIGH)


def three_parts(value):
    upper = value.astype(BF16).astype(F32)
    middle = (value - upper).astype(BF16).astype(F32)
    return jnp.concatenate([upper, middle, value - upper - middle]).astype(BF16)


def first_kernel(
    sel_ref, sketch_ref, e_ref, c_in, inv_ref, d_ref, gamma_ref, image_ref, projected_ref, c_ref, sem
):
    load = pltpu.make_async_copy(c_in, c_ref, sem.at[0])
    load.start()
    sketch = sketch_ref[...]
    picked = jnp.where(selection(sel_ref, sketch.shape[1]), DAMPING, 0.0)

    @pl.when(jnp.min(sel_ref[...].astype(F32)) >= 0.0)
    def _():
        inv_ref[...] = negative_inverse(mul_nt(sketch, sketch + picked, HIGH))

    neg_inv = inv_ref[...]
    direction, gamma = precondition(e_ref[...], sketch, neg_inv)
    d_ref[...] = direction
    gamma_ref[...] = gamma
    load.wait()
    projected = mul_nn(direction.astype(BF16), c_ref[...])
    projected_ref[...] = projected
    nv = direction.shape[0]
    image = mul_nt(three_parts(projected), c_ref[...])
    image_ref[...] = image[:nv] + (image[nv : 2 * nv] + image[2 * nv :])


def second_kernel(
    sum_ref,
    d_ref,
    e_ref,
    inv_ref,
    sketch_ref,
    gamma_ref,
    c_in,
    d1_ref,
    alpha_ref,
    gamma1_ref,
    curv_ref,
    projected_ref,
    c_ref,
    sem,
):
    load = pltpu.make_async_copy(c_in, c_ref, sem.at[0])
    load.start()
    direction, gamma = d_ref[...], gamma_ref[...]
    image = sum_ref[...] + DAMPING * direction
    alpha = solve_small(mul_nt(direction, image, HIGH), gamma)
    alpha_ref[...] = alpha
    residual = e_ref[...] - mul_tn(alpha, image, HIGH)
    result, gamma1 = precondition(residual, sketch_ref[...], inv_ref[...])
    gamma1_ref[...] = gamma1
    direction1 = result + mul_tn(solve_small(gamma, gamma1), direction, HIGH)
    d1_ref[...] = direction1
    nv = direction1.shape[0]
    load.wait()
    parts = mul_nn(three_parts(direction1), c_ref[...])
    projected_ref[...] = parts[:nv]
    curvature = mul_nt(parts[:nv] + (parts[nv : 2 * nv] + parts[2 * nv :]), parts[:nv], HIGH)
    flat = jnp.concatenate([curvature[i : i + 1, :] for i in range(nv)] + [jnp.zeros((1, 128 - nv * nv), F32)], axis=1)
    curv_ref[...] = jnp.broadcast_to(flat[None], curv_ref.shape)


def last_kernel(curv_ref, d_ref, d1_ref, alpha_ref, gamma1_ref, p0_ref, p1_ref, solution_ref, update_ref):
    d1, alpha = d1_ref[...], alpha_ref[...]
    nv = alpha.shape[0]
    flat = jnp.sum(curv_ref[...], axis=0)
    curvature = jnp.concatenate([flat[:, nv * i : nv * i + nv] for i in range(nv)])
    curvature = curvature + DAMPING * mul_nt(d1, d1, HIGH)
    alpha1 = solve_small(curvature, gamma1_ref[...])
    solution_ref[...] = mul_tn(alpha, d_ref[...], HIGH) + mul_tn(alpha1, d1, HIGH)
    both = jnp.concatenate([p0_ref[...], p1_ref[...]])
    update = mul_tn(jnp.concatenate([alpha, alpha1]), both, HIGH).astype(update_ref.dtype)
    for i in range(update_ref.shape[0]):
        update_ref[i] = update


def call(kernel, name, outs, *args, slab=None):
    vmem = pl.BlockSpec(memory_space=pltpu.VMEM)
    held = [] if slab is None else [slab]
    return pl.pallas_call(
        kernel,
        in_specs=[vmem] * len(args) + [pl.BlockSpec(memory_space=pl.ANY)] * len(held),
        out_specs=[vmem] * len(outs),
        out_shape=[jax.ShapeDtypeStruct(shape, dtype) for shape, dtype in outs],
        scratch_shapes=[scratch for x in held for scratch in (pltpu.VMEM(x.shape, x.dtype), pltpu.SemaphoreType.DMA((1,)))],
        compiler_params=pltpu.CompilerParams(vmem_limit_bytes=(46 if held else 24) * 1024 * 1024),
        name=name,
    )(*args, *held)


def body(log_derivs, energies, nys_rows):
    samp_rows, nv = energies.shape
    per_group = nys_rows.shape[1]
    groups = lax.axis_size(SAMP)
    n = samp_rows * groups
    rank = per_group * groups
    devices = lax.axis_size(EVERY)
    total_cols = log_derivs.shape[1] * lax.axis_size(PAR)

    cols = log_derivs.shape[1] // groups
    slab = lax.all_to_all(pack(log_derivs, groups, energies.T, nys_rows), SAMP, 0, 0, tiled=True)
    centered, pieces, e, selected = sketch_call(slab, cols, nv, per_group, 1.0 / math.sqrt(total_cols))
    got = lax.all_to_all(pieces, EVERY, 0, 0, tiled=True)
    own = jnp.sum(got, axis=0)
    pieces = lax.all_to_all(jnp.broadcast_to(own[None], pieces.shape), EVERY, 0, 0, tiled=True)
    sketch = pieces.reshape(rank // 8, n // 128, 8, 128).swapaxes(1, 2).reshape(rank, n)

    vec, mat = ((nv, n), F32), ((nv, nv), F32)
    projected = ((nv, cols), F32)
    neg_inv, d0, gamma0, image, p0 = call(
        first_kernel, "first", [((rank, rank), F32), vec, mat, vec, projected], selected, sketch, e, slab=centered
    )
    image = sum_everywhere(image)
    d1, alpha0, gamma1, curvature, p1 = call(
        second_kernel,
        "second",
        [vec, mat, mat, ((devices, 1, 128), F32), projected],
        image,
        d0,
        e,
        neg_inv,
        sketch,
        gamma0,
        slab=centered,
    )
    start = (lax.axis_index(SAMP) * samp_rows).astype(jnp.uint32)
    curvature, start = lax.optimization_barrier((curvature, start))
    curvature = lax.all_to_all(curvature, EVERY, 0, 0, tiled=True)
    solution, update = call(
        last_kernel, "last", [vec, ((groups, nv, cols), BF16)], curvature, d0, d1, alpha0, gamma1, p0, p1
    )
    own = lax.dynamic_slice(solution, (jnp.uint32(0), start), (nv, samp_rows)).T
    update, own = lax.optimization_barrier((update, own))
    blocks = lax.all_to_all(update, SAMP, 0, 0, tiled=True)
    update = jnp.moveaxis(blocks.astype(F32), 0, 1).reshape(nv, -1).T
    return update, own


def solution(mesh):
    finer = Mesh(mesh.devices.reshape(4, 4, 4, 2), EVERY)
    in_specs = (P(SAMP, PAR), P(SAMP, None), P(SAMP, None))
    out_specs = (P(PAR, None), P(SAMP, None))
    return jax.shard_map(body, mesh=finer, in_specs=in_specs, out_specs=out_specs, check_vma=False)
```

```python
import functools
import math

import jax
import jax.numpy as jnp
from jax import lax
from jax.experimental import pallas as pl
from jax.experimental.pallas import tpu as pltpu
from jax.sharding import Mesh
from jax.sharding import PartitionSpec as P

DAMPING = 0.5
SAMP = ("y", "x")
PAR = ("z", "c")
EVERY = ("y", "x", "z", "c")
F32 = jnp.float32
BF16 = jnp.bfloat16
HIGH = lax.Precision.HIGHEST


def mul_nn(a, b, precision=None):
    return lax.dot_general(a, b, (((1,), (0,)), ((), ())), precision=precision, preferred_element_type=F32)


def mul_nt(a, b, precision=None):
    return lax.dot_general(a, b, (((1,), (1,)), ((), ())), precision=precision, preferred_element_type=F32)


def mul_tn(a, b, precision=None):
    return lax.dot_general(a, b, (((0,), (0,)), ((), ())), precision=precision, preferred_element_type=F32)


def shift(value, axis, by):
    n = lax.axis_size(axis)
    return lax.ppermute(value, axis, [(i, (i + by) % n) for i in range(n)])


def sum_axis(value, axis):
    n = lax.axis_size(axis)
    if n == 2:
        return value + shift(value, axis, 1)
    one, two, three = shift(value, axis, 1), shift(value, axis, 2), shift(value, axis, 3)
    return (value + two) + (one + three)


def sum_everywhere(value):
    for axis in ("c", "x", "y", "z"):
        value = sum_axis(value, axis)
    return value


def eliminate(cols, right, rows):
    b = len(cols)
    cols = list(cols)
    for j in range(b):
        col = cols[j]
        inv = 1.0 / col[j : j + 1, :]
        line = right[j : j + 1, :] * inv
        right = jnp.where(rows == j, line, right - col * line)
        for m in range(j + 1, b):
            line = cols[m][j : j + 1, :] * inv
            cols[m] = jnp.where(rows == j, line, cols[m] - col * line)
    return right


def solve_small(matrix, right):
    b = matrix.shape[0]
    rows = lax.broadcasted_iota(jnp.int32, right.shape, 0)
    cols = [jnp.broadcast_to(matrix[:, m : m + 1], right.shape) for m in range(b)]
    return eliminate(cols, right, rows)


def negative_inverse(a, b=16):
    n = a.shape[0]
    rows = lax.broadcasted_iota(jnp.int32, (b, n), 0)
    lanes = lax.broadcasted_iota(jnp.int32, (b, n), 1)
    all_rows = lax.broadcasted_iota(jnp.int32, (n, n), 0)
    all_lanes = lax.broadcasted_iota(jnp.int32, (n, n), 1)
    for k in range(0, n, b):
        panel = a[k : k + b, :]
        inside = (lanes >= k) & (lanes < k + b)
        left = jnp.where(inside, jnp.where(lanes == rows + k, 1.0, 0.0), panel)
        cols = [jnp.broadcast_to(panel[:, k + m : k + m + 1], (b, n)) for m in range(b)]
        right = eliminate(cols, left, rows)
        touched = ((all_rows >= k) & (all_rows < k + b)) | ((all_lanes >= k) & (all_lanes < k + b))
        a = jnp.where(touched, 0.0, a) - mul_tn(left, right, HIGH)
    return a


def pack_kernel(l_ref, e_in, picks_in, out_ref, e_ref, picks_ref, sems):
    parts, rows, width = out_ref.shape
    width -= 128
    loads = [
        pltpu.make_async_copy(
            l_ref.at[:, pl.ds(i * width, width)], out_ref.at[i, :, pl.ds(0, width)], sems.at[i]
        )
        for i in range(parts)
    ]
    small = [
        pltpu.make_async_copy(e_in, e_ref, sems.at[parts]),
        pltpu.make_async_copy(picks_in, picks_ref, sems.at[parts + 1]),
    ]
    for load in small + loads:
        load.start()
    for load in small:
        load.wait()
    e = e_ref[...]
    nv, group_rows = e.shape
    upper = e.astype(BF16).astype(F32)
    middle = (e - upper).astype(BF16).astype(F32)
    lower = e - upper - middle
    square = (picks_ref.shape[1],) * 2
    diagonal = lax.broadcasted_iota(jnp.int32, square, 0) == lax.broadcasted_iota(jnp.int32, square, 1)
    picks = jnp.broadcast_to(picks_ref[...].astype(F32), square)
    picks = jnp.sum(jnp.where(diagonal, picks, 0.0), axis=1, keepdims=True)
    side = (nv, 128 - group_rows)
    picks = jnp.where(lax.broadcasted_iota(jnp.int32, side, 1) == 0, picks, 0.0)
    none = jnp.zeros(side, F32)
    tile = jnp.concatenate(
        [
            jnp.concatenate([upper, picks], axis=1),
            jnp.concatenate([middle, none], axis=1),
            jnp.concatenate([lower, none], axis=1),
            jnp.zeros((rows - 3 * nv, 128), F32),
        ]
    ).astype(BF16)
    for i in range(parts):
        out_ref[i, :, width:] = tile
    for load in loads:
        load.wait()


def pack(local, parts, energies, picks):
    rows, cols = local.shape[0], local.shape[1] // parts
    vmem = pl.BlockSpec(memory_space=pltpu.VMEM)
    return pl.pallas_call(
        pack_kernel,
        in_specs=[pl.BlockSpec(memory_space=pl.ANY)] * 3,
        out_specs=vmem,
        out_shape=jax.ShapeDtypeStruct((parts, rows, cols + 128), BF16),
        scratch_shapes=[
            pltpu.VMEM(energies.shape, F32),
            pltpu.VMEM(picks.shape, jnp.int32),
            pltpu.SemaphoreType.DMA((parts + 2,)),
        ],
        compiler_params=pltpu.CompilerParams(vmem_limit_bytes=60 * 1024 * 1024),
        name="pack",
    )(local, energies, picks)


def selection(sel_ref, n):
    return lax.broadcasted_iota(jnp.int32, (sel_ref.shape[0], n), 1) == sel_ref[...]


def sketch_kernel(
    scale, slab_in, c_out, sketch_ref, e_ref, sel_ref, slab_ref, c_ref, pick_ref, acc_ref, sems, load_sems
):
    groups, rows, _ = slab_ref.shape
    cols = c_out.shape[1]
    width = min(512, cols)
    windows = [(cols, 128)] + [(start, width) for start in range(0, cols, width)]
    loads = [
        pltpu.make_async_copy(
            slab_in.at[:, :, pl.ds(start, size)], slab_ref.at[:, :, pl.ds(start, size)], load_sems.at[i]
        )
        for i, (start, size) in enumerate(windows)
    ]
    for load in loads:
        load.start()
    loads.pop(0).wait()
    n = groups * rows
    nv = e_ref.shape[0]
    for i in range(groups):
        tile = slab_ref[i, 0:32, cols:].astype(F32)
        upper, middle, lower = tile[0:nv], tile[nv : 2 * nv], tile[2 * nv : 3 * nv]
        e_ref[:, i * rows : (i + 1) * rows] = (upper + (middle + lower))[:, :rows]
        sel_ref[i * nv : (i + 1) * nv, :] = upper[:, rows : rows + 1].astype(jnp.int32) + i * rows
    pick_ref[...] = jnp.where(selection(sel_ref, n), 1.0, 0.0).astype(BF16)
    stores = []
    for start in range(0, cols, width):
        place = slice(start, start + width)
        loads[start // width].wait()
        total = 0.0
        for i in range(groups):
            total = total + jnp.sum(slab_ref[i, :, place].astype(F32), axis=0, keepdims=True)
        mean = total / n
        for i in range(groups):
            c_ref[i * rows : (i + 1) * rows, place] = ((slab_ref[i, :, place].astype(F32) - mean) * scale).astype(BF16)
        window = pl.ds(start, width)
        stores.append(
            pltpu.make_async_copy(c_ref.at[:, window], c_out.at[:, window], sems.at[start // width])
        )
        stores[-1].start()
        chosen = mul_nn(pick_ref[...], c_ref[:, place]).astype(BF16)
        product = mul_nt(chosen, c_ref[:, place])
        acc_ref[...] = product if start == 0 else acc_ref[...] + product
    for i in range(0, acc_ref.shape[0], 8):
        for j in range(0, n, 128):
            sketch_ref[i * n // 1024 + j // 128] = acc_ref[i : i + 8, j : j + 128]
    for store in stores:
        store.wait()


def sketch_call(slab, cols, nv, per_group, scale):
    groups, rows, _ = slab.shape
    rank, n = per_group * groups, groups * rows
    return pl.pallas_call(
        functools.partial(sketch_kernel, scale),
        in_specs=[pl.BlockSpec(memory_space=pl.ANY)],
        out_specs=[pl.BlockSpec(memory_space=pl.ANY)] + [pl.BlockSpec(memory_space=pltpu.VMEM)] * 3,
        out_shape=[
            jax.ShapeDtypeStruct((n, cols), BF16),
            jax.ShapeDtypeStruct((rank * n // 1024, 8, 128), F32),
            jax.ShapeDtypeStruct((nv, n), F32),
            jax.ShapeDtypeStruct((rank, 1), jnp.int32),
        ],
        scratch_shapes=[
            pltpu.VMEM(slab.shape, BF16),
            pltpu.VMEM((n, cols), BF16),
            pltpu.VMEM((rank, n), BF16),
            pltpu.VMEM((rank, n), F32),
            pltpu.SemaphoreType.DMA((-(-cols // 512),)),
            pltpu.SemaphoreType.DMA((-(-cols // 512) + 1,)),
        ],
        compiler_params=pltpu.CompilerParams(vmem_limit_bytes=46 * 1024 * 1024),
        name="sketch",
    )(slab)


def precondition(residual, sketch, neg_inv):
    coeffs = mul_nn(mul_nt(residual, sketch, HIGH), neg_inv, HIGH)
    result = (residual + mul_nn(coeffs, sketch, HIGH)) / DAMPING
    return result, mul_nt(result, residual, HIGH)


def three_parts(value):
    upper = value.astype(BF16).astype(F32)
    middle = (value - upper).astype(BF16).astype(F32)
    return jnp.concatenate([upper, middle, value - upper - middle]).astype(BF16)


def first_kernel(
    sel_ref, sketch_ref, e_ref, c_in, inv_ref, d_ref, gamma_ref, image_ref, projected_ref, c_ref, sem
):
    load = pltpu.make_async_copy(c_in, c_ref, sem.at[0])
    load.start()
    sketch = sketch_ref[...]
    picked = jnp.where(selection(sel_ref, sketch.shape[1]), DAMPING, 0.0)

    @pl.when(jnp.min(sel_ref[...].astype(F32)) >= 0.0)
    def _():
        inv_ref[...] = negative_inverse(mul_nt(sketch, sketch + picked, HIGH))

    neg_inv = inv_ref[...]
    direction, gamma = precondition(e_ref[...], sketch, neg_inv)
    d_ref[...] = direction
    gamma_ref[...] = gamma
    load.wait()
    projected = mul_nn(direction.astype(BF16), c_ref[...])
    projected_ref[...] = projected
    nv = direction.shape[0]
    image = mul_nt(three_parts(projected), c_ref[...])
    image_ref[...] = image[:nv] + (image[nv : 2 * nv] + image[2 * nv :])


def second_kernel(
    sum_ref,
    d_ref,
    e_ref,
    inv_ref,
    sketch_ref,
    gamma_ref,
    c_in,
    d1_ref,
    alpha_ref,
    gamma1_ref,
    curv_ref,
    projected_ref,
    c_ref,
    sem,
):
    load = pltpu.make_async_copy(c_in, c_ref, sem.at[0])
    load.start()
    direction, gamma = d_ref[...], gamma_ref[...]
    image = sum_ref[...] + DAMPING * direction
    alpha = solve_small(mul_nt(direction, image, HIGH), gamma)
    alpha_ref[...] = alpha
    residual = e_ref[...] - mul_tn(alpha, image, HIGH)
    result, gamma1 = precondition(residual, sketch_ref[...], inv_ref[...])
    gamma1_ref[...] = gamma1
    direction1 = result + mul_tn(solve_small(gamma, gamma1), direction, HIGH)
    d1_ref[...] = direction1
    nv = direction1.shape[0]
    load.wait()
    parts = mul_nn(three_parts(direction1), c_ref[...])
    projected_ref[...] = parts[:nv]
    curvature = mul_nt(parts[:nv] + (parts[nv : 2 * nv] + parts[2 * nv :]), parts[:nv], HIGH)
    flat = jnp.concatenate([curvature[i : i + 1, :] for i in range(nv)] + [jnp.zeros((1, 128 - nv * nv), F32)], axis=1)
    curv_ref[...] = jnp.broadcast_to(flat[None], curv_ref.shape)


def last_kernel(curv_ref, d_ref, d1_ref, alpha_ref, gamma1_ref, p0_ref, p1_ref, solution_ref, update_ref):
    d1, alpha = d1_ref[...], alpha_ref[...]
    nv = alpha.shape[0]
    flat = jnp.sum(curv_ref[...], axis=0)
    curvature = jnp.concatenate([flat[:, nv * i : nv * i + nv] for i in range(nv)])
    curvature = curvature + DAMPING * mul_nt(d1, d1, HIGH)
    alpha1 = solve_small(curvature, gamma1_ref[...])
    solution_ref[...] = mul_tn(alpha, d_ref[...], HIGH) + mul_tn(alpha1, d1, HIGH)
    both = jnp.concatenate([p0_ref[...], p1_ref[...]])
    update = mul_tn(jnp.concatenate([alpha, alpha1]), both, HIGH).astype(update_ref.dtype)
    for i in range(update_ref.shape[0]):
        update_ref[i] = update


def call(kernel, name, outs, *args, slab=None):
    vmem = pl.BlockSpec(memory_space=pltpu.VMEM)
    held = [] if slab is None else [slab]
    return pl.pallas_call(
        kernel,
        in_specs=[vmem] * len(args) + [pl.BlockSpec(memory_space=pl.ANY)] * len(held),
        out_specs=[vmem] * len(outs),
        out_shape=[jax.ShapeDtypeStruct(shape, dtype) for shape, dtype in outs],
        scratch_shapes=[scratch for x in held for scratch in (pltpu.VMEM(x.shape, x.dtype), pltpu.SemaphoreType.DMA((1,)))],
        compiler_params=pltpu.CompilerParams(vmem_limit_bytes=(46 if held else 24) * 1024 * 1024),
        name=name,
    )(*args, *held)


def body(log_derivs, energies, nys_rows):
    samp_rows, nv = energies.shape
    per_group = nys_rows.shape[1]
    groups = lax.axis_size(SAMP)
    n = samp_rows * groups
    rank = per_group * groups
    devices = lax.axis_size(EVERY)
    total_cols = log_derivs.shape[1] * lax.axis_size(PAR)

    cols = log_derivs.shape[1] // groups
    slab = lax.all_to_all(pack(log_derivs, groups, energies.T, nys_rows), SAMP, 0, 0, tiled=True)
    centered, pieces, e, selected = sketch_call(slab, cols, nv, per_group, 1.0 / math.sqrt(total_cols))
    got = lax.all_to_all(pieces, EVERY, 0, 0, tiled=True)
    own = jnp.sum(got, axis=0)
    pieces = lax.all_to_all(jnp.broadcast_to(own[None], pieces.shape), EVERY, 0, 0, tiled=True)
    sketch = pieces.reshape(rank // 8, n // 128, 8, 128).swapaxes(1, 2).reshape(rank, n)

    vec, mat = ((nv, n), F32), ((nv, nv), F32)
    projected = ((nv, cols), F32)
    neg_inv, d0, gamma0, image, p0 = call(
        first_kernel, "first", [((rank, rank), F32), vec, mat, vec, projected], selected, sketch, e, slab=centered
    )
    image = sum_everywhere(image)
    d1, alpha0, gamma1, curvature, p1 = call(
        second_kernel,
        "second",
        [vec, mat, mat, ((devices, 1, 128), F32), projected],
        image,
        d0,
        e,
        neg_inv,
        sketch,
        gamma0,
        slab=centered,
    )
    start = (lax.axis_index(SAMP) * samp_rows).astype(jnp.uint32)
    curvature, start = lax.optimization_barrier((curvature, start))
    curvature = lax.all_to_all(curvature, EVERY, 0, 0, tiled=True)
    solution, update = call(
        last_kernel, "last", [vec, ((groups, nv, cols), BF16)], curvature, d0, d1, alpha0, gamma1, p0, p1
    )
    own = lax.dynamic_slice(solution, (jnp.uint32(0), start), (nv, samp_rows)).T
    update, own = lax.optimization_barrier((update, own))
    blocks = lax.all_to_all(update, SAMP, 0, 0, tiled=True)
    update = jnp.moveaxis(blocks.astype(F32), 0, 1).reshape(nv, -1).T
    return update, own


def solution(mesh):
    finer = Mesh(mesh.devices.reshape(4, 4, 4, 2), EVERY)
    in_specs = (P(SAMP, PAR), P(SAMP, None), P(SAMP, None))
    out_specs = (P(PAR, None), P(SAMP, None))
    return jax.shard_map(body, mesh=finer, in_specs=in_specs, out_specs=out_specs, check_vma=False)
```
